256 devices in a mesh: dp: 32 (over z, y), tp: 8 (over x, core).
Axes of the slice: x: 4, y: 4, z: 8, core: 2. Of those that a mesh axis runs over, the one named last changes fastest.
Arguments:
- tokens: bfloat16 [16384, 2560], P('dp', 'tp'), may hold values from -20 to 20
- pre_act: bfloat16 [16384, 10240], P('dp', 'tp'), may hold values from -6 to 6
- act_grad: bfloat16 [16384, 10240], P('dp', 'tp'), may hold values from -3 to 3
Outputs:
- slab_gradient: bfloat16 [2560, 10240], P(None, 'tp')
The draws below stay inside these ranges and needn't reach their ends.
All inputs are finite; a program needn't handle non-finite values.
Results may differ from the reference program's by a relative error of at most 0.0052.
Values may be sent and summed in bfloat16 or wider, within the bound.
A program may use at most 64 MiB of HBM per device.

```python
import jax
import jax.numpy as jnp
from jax import lax

D = 2560
FF = 10240
TOK_DEV = 512
TOKENS = 16384
N_DP = 32


def draw_tokens(key, part):
    key = jax.random.fold_in(key, 11)
    key_base, key_offset, key_scale = jax.random.split(key, 3)
    position = jnp.arange(D, dtype=jnp.float32) / D
    base = jnp.clip(jax.random.normal(key_base, (TOKENS, D), jnp.float32), -6.0, 6.0)
    offset = jax.random.uniform(key_offset, (D,), jnp.float32, -0.8, 0.8)
    offset = jnp.where(position < 0.5, offset, 0.0)
    column_scale = 10.0 ** position * jax.random.uniform(key_scale, (D,), jnp.float32, 0.5, 1.0)
    return ((base + offset[None, :]) * column_scale[None, :] * 0.25).astype(jnp.bfloat16)


def draw_act_grad(key, part):
    key = jax.random.fold_in(key, 12)
    key_base, key_offset, key_scale = jax.random.split(key, 3)
    position = jnp.arange(FF, dtype=jnp.float32) / FF
    row_place = jnp.arange(TOKENS, dtype=jnp.float32) / TOKENS
    base = jnp.clip(jax.random.normal(key_base, (TOKENS, FF), jnp.float32), -6.0, 6.0)
    offset = jax.random.uniform(key_offset, (FF,), jnp.float32, -0.6, 0.6)
    offset = jnp.where(position >= 0.5, offset, 0.0)
    column_scale = 10.0 ** position * jax.random.uniform(key_scale, (FF,), jnp.float32, 0.5, 1.0)
    row_scale = 3.0 ** row_place
    factor = 0.3 / TOK_DEV ** 0.5
    values = (base + offset[None, :]) * column_scale[None, :] * row_scale[:, None] * factor
    return jnp.clip(values, -3.0, 3.0).astype(jnp.bfloat16)


def block_scale(stream_key, extent, cuts, smallest, largest):
    gain = 1.0
    for dim, parts in cuts:
        draws = jax.random.uniform(jax.random.fold_in(jax.random.fold_in(stream_key, 6), dim), (parts,), jnp.float32, smallest / len(cuts), largest / len(cuts))
        gain = gain * jnp.repeat(jnp.exp(draws), extent[dim] // parts).reshape((-1,) + (1,) * (len(extent) - 1 - dim))
    return gain


def bell_draw(own_key, shape, deviation, most, cuts=(), kind=jnp.bfloat16):
    drawn = deviation * jax.random.normal(own_key, shape, jnp.float32)
    if cuts:
        drawn = drawn * block_scale(own_key, shape, cuts, -0.22, 0.18)
    return jnp.clip(drawn, -most, most).astype(kind)


def setup_inputs(seed: int = 0) -> dict:
    arg_keys = jax.random.split(jax.random.key(seed), 4)
    return {
        "tokens": draw_tokens(jax.random.fold_in(arg_keys[3], 71), 0),
        "pre_act": bell_draw(arg_keys[1], (TOKENS, FF), 1.5, 6.0, ((0, 32), (1, 8))),
        "act_grad": draw_act_grad(jax.random.fold_in(arg_keys[3], 71), 0),
    }


norm_epsilon = 1e-6
gelu_scale = 0.7978845608


def gelu_slope(values):
    inner = gelu_scale * (values + 0.044715 * values * values * values)
    tangent = jnp.tanh(inner)
    return 0.5 * (1.0 + tangent) + 0.5 * values * (1.0 - tangent * tangent) * gelu_scale * (1.0 + 0.134145 * values * values)


def adasum_pair(first_sum, second_sum):
    left_part = first_sum.astype(jnp.float32)
    right_part = second_sum.astype(jnp.float32)
    inner_prod = jnp.sum(left_part * right_part)
    left_norm = jnp.sum(left_part * left_part)
    right_norm = jnp.sum(right_part * right_part)
    left_coef = 1.0 - inner_prod / (2.0 * (left_norm + norm_epsilon))
    right_coef = 1.0 - inner_prod / (2.0 * (right_norm + norm_epsilon))
    return (left_coef * left_part + right_coef * right_part).astype(jnp.bfloat16)


def reference(tokens, pre_act, act_grad):
    derivative = gelu_slope(pre_act.astype(jnp.float32))
    grad_pre = (act_grad.astype(jnp.float32) * derivative).astype(jnp.bfloat16)

    def replica_gradient(replica):
        rows_in = tokens[replica * TOK_DEV:(replica + 1) * TOK_DEV]
        rows_out = grad_pre[replica * TOK_DEV:(replica + 1) * TOK_DEV]
        product = lax.dot_general(rows_in, rows_out, (((0,), (0,)), ((), ())), preferred_element_type=jnp.float32)
        return product.astype(jnp.bfloat16)

    def combine_tree(offset, stride):
        if stride == N_DP:
            return replica_gradient(offset)
        lower_tree = combine_tree(offset, 2 * stride)
        upper_tree = combine_tree(offset + stride, 2 * stride)
        return adasum_pair(lower_tree, upper_tree)

    return combine_tree(0, 1)
```

```python
import jax
import jax.numpy as jnp
from jax import lax
from jax.experimental import pallas as pl
from jax.experimental.pallas import tpu as pltpu
from jax.sharding import PartitionSpec as P

norm_epsilon = 1e-06
gelu_scale = 0.7978845608
MESH = pl.DeviceIdType.MESH
NX, NY, NZ = 4, 4, 8
SEND_SEMS = 192


def gelu_slope(values):
    inner = gelu_scale * (values + 0.044715 * values * values * values)
    tangent = jnp.tanh(inner)
    return 0.5 * (1.0 + tangent) + 0.5 * values * (1.0 - tangent * tangent) * gelu_scale * (
        1.0 + 0.134145 * values * values
    )


def signed(step):
    return step if step <= NZ // 2 else step - NZ


def tree_weights(gram, strides):
    shape = gram.shape
    row = lax.broadcasted_iota(jnp.int32, shape, 0)
    lane = lax.broadcasted_iota(jnp.int32, shape, 1)
    own = lane % 8 == row
    first = lane < 8
    weight = jnp.ones((8, 1), jnp.float32)
    for stride in strides:
        pair = lane % 8 == (row + stride) % 8
        own_col = jnp.sum(jnp.where(own & first, gram, 0.0), axis=1, keepdims=True)
        pair_col = jnp.sum(jnp.where(pair & first, gram, 0.0), axis=1, keepdims=True)
        own_row = jnp.sum(jnp.where(own, gram, 0.0), axis=0, keepdims=True)
        pair_row = jnp.sum(
            jnp.where(row == (lane + stride) % 8, gram, 0.0), axis=0, keepdims=True
        )
        coef_col = 1.0 - pair_col / (2.0 * (jnp.maximum(own_col, 0.0) + norm_epsilon))
        coef_row = 1.0 - pair_row / (2.0 * (jnp.maximum(own_row, 0.0) + norm_epsilon))
        weight = weight * coef_col
        scaled = gram * coef_col * coef_row
        scaled = scaled + pltpu.roll(scaled, stride, 0)
        gram = scaled + pltpu.roll(scaled, stride, 1)
    return weight


def fold_gram(product, count, group):
    size = count * group
    row = lax.broadcasted_iota(jnp.int32, (size, size), 0)
    lane = lax.broadcasted_iota(jnp.int32, (size, size), 1)
    kept = jnp.where(row % group == lane % group, product, 0.0)
    rows = jnp.sum(kept.reshape(count, group, size), axis=1)
    lane = lax.broadcasted_iota(jnp.int32, (count, size), 1)
    out_lane = lax.broadcasted_iota(jnp.int32, (count, 128), 1)
    total = jnp.zeros((count, 128), jnp.float32)
    for index in range(count):
        one = jnp.sum(jnp.where(lane // group == index, rows, 0.0), axis=1, keepdims=True)
        total = jnp.where(out_lane % count == index, one, total)
    return total


def kernel(
    xt, pre, act, out,
    xb, yb, ys, pre_v, act_v, grads, prod, vs, vr, fin,
    a1, a2, b1, b2,
    load_sem, send_sem, xz_sem, xx_sem, yz_sem, yy_sem, v_sem, ar_sem,
    bz_sem, by_sem, az_sem, ay_sem,
):
    dp, tp = lax.axis_index("dp"), lax.axis_index("tp")
    z, y, x, c = dp // NY, dp % NY, tp // 2, tp % 2
    tokens = yb.shape[1]
    half_tok = tokens // 2
    feats = xb.shape[2]
    cols = yb.shape[2]

    def dev(x_, c_, y_, z_):
        return (z_ * NY + y_, x_ * 2 + c_)

    def zn(step):
        return (z + step + NZ) % NZ

    def yn(step):
        return (y + step + NY) % NY

    def xn(step):
        return (x + step + NX) % NX

    pending = []
    counter = [0]

    def send(src, dst, recv, device, cond=None, size=None):
        copy = pltpu.make_async_remote_copy(
            src_ref=src, dst_ref=dst, send_sem=send_sem.at[counter[0]], recv_sem=recv,
            device_id=device, device_id_type=MESH,
        )
        if cond is None:
            copy.start()
        else:
            pl.when(cond)(copy.start)
        pending.append((size or (lambda: src), counter[0], cond))
        counter[0] += 1

    def arrived(ref, sem):
        pltpu.make_async_copy(ref, ref, sem).wait()

    def drain(items):
        for ref, index, cond in items:
            if cond is None:
                arrived(ref(), send_sem.at[index])
            else:
                pl.when(cond)(lambda: arrived(ref(), send_sem.at[index]))

    loads = [
        pltpu.make_async_copy(pre, pre_v, load_sem.at[0]),
        pltpu.make_async_copy(act, act_v, load_sem.at[1]),
    ]
    for load in loads:
        load.start()

    barrier = pltpu.get_barrier_semaphore()
    partners = [dev(x, k, y, zn(s)) for s in range(1, NZ) for k in range(2)]
    partners += [dev(x, 1 - c, y, z)]
    partners += [dev(xn(s), k, y, z) for s in range(1, NX) for k in range(2)]
    partners += [dev(x, k, yn(s), z) for s in range(1, NY) for k in range(2)]
    partners += [dev(xn(s), c, yn(t), z) for s in range(1, NX) for t in range(1, NY)]
    for partner in partners:
        pl.semaphore_signal(barrier, inc=1, device_id=partner, device_id_type=MESH)
    pl.semaphore_wait(barrier, len(partners))

    match = z % 2 == c
    reach = jnp.where(match, 2, 1)
    for sign in (1, -1):
        for k in range(2):
            send(
                xt.at[pl.ds(k * feats, feats)], xb.at[z, x], xz_sem.at[z],
                dev(x, k, y, (z + sign * reach + NZ) % NZ),
            )
    other = pl.multiple_of((1 - c) * feats, 16)
    mine = pl.multiple_of(c * feats, 16)
    own_x = pltpu.make_async_copy(xt.at[pl.ds(mine, feats)], xb.at[z, x], xz_sem.at[z])
    pl.when(match)(own_x.start)
    send(xt.at[pl.ds(other, feats)], xb.at[z, x], xz_sem.at[z], dev(x, 1 - c, y, z), match)

    for load in loads:
        load.wait()
    chunk = 32
    my_pair, my_parity = z // 2, z % 2
    for j in range(2):
        def slope_rows(i, carry):
            rows = pl.ds(pl.multiple_of(i * chunk, chunk), chunk)
            span = pl.ds(j * cols, cols)
            slope = gelu_slope(pre_v[rows, span].astype(jnp.float32))
            ys[j, rows, :] = (act_v[rows, span].astype(jnp.float32) * slope).astype(jnp.bfloat16)
            return carry

        lax.fori_loop(0, tokens // chunk, slope_rows, 0)
        quarter = 2 * c + j
        ahead = (quarter - my_pair + 4) % 4
        upper = jnp.where(
            ahead == 0, 1 - my_parity,
            jnp.where(ahead == 3, 1, jnp.where(ahead == 2, 1 - my_parity, 0)),
        )
        target = 2 * quarter + upper
        for k in range(2):
            rows = pl.ds(k * half_tok, half_tok)
            send(ys.at[j, rows], yb.at[z, rows], yz_sem.at[z], dev(x, k, y, target))
        own = ahead == 0
        own_rows = pl.ds(pl.multiple_of(c * half_tok, 16), half_tok)
        other_rows = pl.ds(pl.multiple_of((1 - c) * half_tok, 16), half_tok)
        own_y = pltpu.make_async_copy(ys.at[j, own_rows], yb.at[z, own_rows], yz_sem.at[z])
        pl.when(own)(own_y.start)
        send(ys.at[j, other_rows], yb.at[z, other_rows], yz_sem.at[z], dev(x, 1 - c, y, z), own)

    def ev_xz(step):
        src = zn(-step)
        piece = xb.at[src, x]
        arrived(piece, xz_sem.at[src])
        if step == 1:
            send(piece, piece, xz_sem.at[src], dev(x, c, y, zn(2)))
        if step == -1:
            send(piece, piece, xz_sem.at[src], dev(x, c, y, zn(-2)))
        if step == 2:
            send(piece, piece, xz_sem.at[src], dev(x, c, y, zn(2)), c == 0)
        if step == -2:
            send(piece, piece, xz_sem.at[src], dev(x, c, y, zn(-2)), c == 1)
        send(piece, piece, xx_sem.at[src, 0], dev(xn(1), c, y, z))
        send(piece, piece, xx_sem.at[src, 1], dev(xn(-1), c, y, z))

    low, high = pl.ds(0, feats // 2), pl.ds(feats // 2, feats // 2)

    def ev_xx(step):
        src = zn(-step)
        left, right = xb.at[src, xn(-1)], xb.at[src, xn(1)]
        arrived(left, xx_sem.at[src, 0])
        send(left.at[low], left.at[low], xx_sem.at[src, 2], dev(xn(1), c, y, z))
        arrived(right, xx_sem.at[src, 1])
        send(right.at[high], right.at[high], xx_sem.at[src, 3], dev(xn(-1), c, y, z))

    my_tok = pl.ds(pl.multiple_of(c * half_tok, 16), half_tok)
    its_tok = pl.ds(pl.multiple_of((1 - c) * half_tok, 16), half_tok)

    def ev_yz(step):
        src = zn(-step)
        piece = yb.at[src, my_tok]
        arrived(piece, yz_sem.at[src])
        if step in (1, 2, 3):
            send(piece, piece, yz_sem.at[src], dev(x, c, y, zn(1)), z % 2 == 0)
        if step in (-1, -2, -3):
            send(piece, piece, yz_sem.at[src], dev(x, c, y, zn(-1)), z % 2 == 1)
        send(piece, piece, yy_sem.at[src], dev(x, 1 - c, y, z))

    def ev_mm(step):
        src = zn(-step)
        far = xb.at[src, xn(2)]
        arrived(far.at[low], xx_sem.at[src, 2])
        arrived(far.at[high], xx_sem.at[src, 3])
        arrived(yb.at[src, its_tok], yy_sem.at[src])

        def block(i, carry):
            result = jnp.dot(xb[src, i], yb[src], preferred_element_type=jnp.float32)
            grads[src, pl.ds(pl.multiple_of(i * feats, 16), feats), :] = result.astype(jnp.bfloat16)
            return carry

        lax.fori_loop(0, NX, block, 0)

    xz, xx, yz, mm = ev_xz, ev_xx, ev_yz, ev_mm
    for event, step in [
        (xz, 0), (xz, 1), (xz, -1), (xx, 0), (xz, 2), (xz, -2), (xx, 1), (xx, -1),
        (yz, 0), (yz, 1), (yz, -1), (xx, 2), (xx, -2), (xz, 3), (xz, -3), (xz, 4), (mm, 0),
        (yz, 2), (yz, -2), (xx, 3), (xx, -3), (mm, 1), (mm, -1), (yz, 3), (yz, -3), (xx, 4),
        (mm, 2), (mm, -2), (yz, 4), (mm, 3), (mm, -3), (mm, 4),
    ]:
        event(step)

    group = 32
    total_rows = grads.shape[1]
    prod[...] = jnp.zeros_like(prod)

    def gram_rows(i, carry):
        rows = pl.ds(pl.multiple_of(i * group, group), group)
        stacked = grads[:, rows, :].reshape(NZ * group, cols)
        prod[...] += lax.dot_general(
            stacked, stacked, (((1,), (1,)), ((), ())), preferred_element_type=jnp.float32
        )
        return carry

    lax.fori_loop(0, total_rows // group, gram_rows, 0)
    a1[tp] = fold_gram(prod[...], NZ, group)
    for s in range(1, 2 * NX):
        send(a1.at[tp], a1.at[tp], ar_sem.at[0], (dp, (tp + s) % (2 * NX)))
    sent = pl.ds(0, 2 * NX - 1)
    arrived(a1.at[sent], ar_sem.at[0])
    a2[z] = jnp.sum(a1[...], axis=0)
    for s in range(1, NZ):
        send(a2.at[z], a2.at[z], ar_sem.at[1], dev(x, c, y, zn(s)))
    drain(pending)
    pending.clear()
    arrived(a2.at[pl.ds(0, NZ - 1)], ar_sem.at[1])
    weight = tree_weights(jnp.sum(a2[...], axis=0), (4, 2, 1))

    owner = z // 4
    is_owner = c == owner
    its_rows = pl.ds(pl.multiple_of(c * feats, 16), feats)
    small = 32
    for s in (1, -1, 2, 0):
        part = yn(s)

        def combine_rows(i, carry):
            total = jnp.zeros((small, cols), jnp.float32)
            rows = pl.ds(pl.multiple_of(part * feats + i * small, 32), small)
            for r in range(NZ):
                total += weight[r:r + 1, :] * grads[r, rows, :].astype(jnp.float32)
            vs[part, pl.ds(pl.multiple_of(i * small, small), small), :] = total.astype(jnp.bfloat16)
            return carry

        lax.fori_loop(0, feats // small, combine_rows, 0)
        if s:
            send(vs.at[part], vr.at[y, its_rows], v_sem.at[y, c], dev(x, owner, part, z))
        else:
            own_v = pltpu.make_async_copy(vs.at[part], vr.at[y, its_rows], v_sem.at[y, c])
            pl.when(is_owner)(own_v.start)
            send(vs.at[part], vr.at[y, its_rows], v_sem.at[y, c], dev(x, owner, part, z),
                 jnp.logical_not(is_owner))

    block_rows = 2 * feats
    cut = block_rows * 2 // 5
    part_a, part_b = (0, cut), (cut, block_rows - cut)

    def place(y_, z_, start, size):
        top = pl.multiple_of((2 * y_ + z_ % 2) * block_rows + start, 16)
        left = pl.multiple_of((z_ // 2) % 2 * cols, 128)
        return out.at[pl.ds(top, size), pl.ds(left, cols)]

    def halves(part):
        start, size = part
        return (start, size // 2), (start + size // 2, size // 2)

    def finish():
        for src in range(NY):
            for k in range(2):
                arrived(vr.at[src, pl.ds(k * feats, feats)], v_sem.at[src, k])
        size = NY * group
        prod[0:size, 0:size] = jnp.zeros((size, size), jnp.float32)

        def gram(i, carry):
            rows = pl.ds(pl.multiple_of(i * group, group), group)
            stacked = vr[:, rows, :].reshape(size, cols)
            prod[0:size, 0:size] += lax.dot_general(
                stacked, stacked, (((1,), (1,)), ((), ())), preferred_element_type=jnp.float32
            )
            return carry

        lax.fori_loop(0, block_rows // group, gram, 0)
        folded = fold_gram(prod[0:size, 0:size], NY, group)
        me = x * NY + y
        b1[me] = jnp.concatenate([folded, folded], axis=0)
        for s in range(NX):
            for t in range(NY):
                if s or t:
                    send(b1.at[me], b1.at[me], ar_sem.at[2], dev(xn(s), c, yn(t), z), size=lambda: b1.at[0])
        arrived(b1.at[pl.ds(0, NX * NY - 1)], ar_sem.at[2])
        b2[z] = jnp.sum(b1[...], axis=0)
        for s in range(1, NZ):
            send(b2.at[z], b2.at[z], ar_sem.at[3], dev(x, zn(s) // 4, y, zn(s)), size=lambda: b2.at[0])
        arrived(b2.at[pl.ds(0, NZ - 1)], ar_sem.at[3])
        last = tree_weights(jnp.sum(b2[...], axis=0), (2, 1))

        def final_rows(i, carry):
            total = jnp.zeros((small, cols), jnp.float32)
            rows = pl.ds(pl.multiple_of(i * small, small), small)
            for r in range(NY):
                total += last[r:r + 1, :] * vr[r, rows, :].astype(jnp.float32)
            fin[rows, :] = total.astype(jnp.bfloat16)
            return carry

        lax.fori_loop(0, block_rows // small, final_rows, 0)
        for part, zs, yidx in ((part_a, az_sem, True), (part_b, bz_sem, False)):
            source = fin.at[pl.ds(*part)]
            goal = place(y, z, *part)
            for s in (1, -1):
                sem = az_sem.at[y, s % NZ] if yidx else bz_sem.at[s % NZ]
                size = lambda part=part: fin.at[pl.ds(*part)]
                send(source, goal, sem, dev(x, c, y, zn(s)), size=size)
                sem = ay_sem.at[0 if s > 0 else 1] if yidx else by_sem.at[0, 0 if s > 0 else 1]
                send(source, goal, sem, dev(x, c, yn(s), z), size=size)
        pltpu.make_async_copy(fin, place(y, z, 0, block_rows), load_sem.at[0]).start()

    mark = len(pending)
    pl.when(is_owner)(finish)
    pending[mark:] = [(ref, index, is_owner) for ref, index, _ in pending[mark:]]

    def z_forward(step, src_y, part, sems, cond):
        src = zn(-step)
        first, second = halves(part)
        if step in (1, 2):
            ref = place(src_y, src, *part)
            send(ref, ref, sems(step + 1), dev(x, c, y, zn(1)), cond)
        elif step in (-1, -2):
            ref = place(src_y, src, *part)
            send(ref, ref, sems((step - 1) % NZ), dev(x, c, y, zn(-1)), cond)
        elif step == 3:
            ref = place(src_y, src, *first)
            send(ref, ref, sems(4), dev(x, c, y, zn(1)), cond)
        elif step == -3:
            ref = place(src_y, src, *second)
            send(ref, ref, sems(0), dev(x, c, y, zn(-1)), cond)

    def z_arrived(step, src_y, part, sems):
        src = zn(-step)
        first, second = halves(part)
        if step == 4:
            arrived(place(src_y, src, *first), sems(4))
            arrived(place(src_y, src, *second), sems(0))
        else:
            arrived(place(src_y, src, *part), sems(step % NZ))

    def member(step):
        return zn(-step) // 4 == c

    def when(cond, task):
        pl.when(cond)(task)

    def ev_bz(step):
        cond = member(step)
        when(cond, lambda: z_arrived(step, y, part_b, lambda i: bz_sem.at[i]))
        z_forward(step, y, part_b, lambda i: bz_sem.at[i], cond)
        ref = place(y, zn(-step), *part_b)
        send(ref, ref, by_sem.at[step % NZ, 0], dev(x, c, yn(1), z), cond)
        send(ref, ref, by_sem.at[step % NZ, 1], dev(x, c, yn(-1), z), cond)

    def spread_y(sem, part, src_z, cond):
        first, second = halves(part)
        left, right = place(yn(-1), src_z, *part), place(yn(1), src_z, *part)
        when(cond, lambda: arrived(left, sem(0)))
        ref = place(yn(-1), src_z, *first)
        send(ref, ref, sem(2), dev(x, c, yn(1), z), cond)
        when(cond, lambda: arrived(right, sem(1)))
        ref = place(yn(1), src_z, *second)
        send(ref, ref, sem(3), dev(x, c, yn(-1), z), cond)

    def ev_by(step):
        spread_y(lambda i: by_sem.at[step % NZ, i], part_b, zn(-step), member(step))

    def ev_byend(step):
        first, second = halves(part_b)
        cond = member(step)
        when(cond, lambda: arrived(place(yn(2), zn(-step), *first), by_sem.at[step % NZ, 2]))
        when(cond, lambda: arrived(place(yn(2), zn(-step), *second), by_sem.at[step % NZ, 3]))

    def ev_ay():
        spread_y(lambda i: ay_sem.at[i], part_a, z, is_owner)
        for s in (1, -1):
            ref = place(yn(-s), z, *part_a)
            send(ref, ref, az_sem.at[yn(-s), 1], dev(x, c, y, zn(1)), is_owner)
            send(ref, ref, az_sem.at[yn(-s), NZ - 1], dev(x, c, y, zn(-1)), is_owner)

    def ev_ayend():
        first, second = halves(part_a)
        when(is_owner, lambda: arrived(place(yn(2), z, *first), ay_sem.at[2]))
        when(is_owner, lambda: arrived(place(yn(2), z, *second), ay_sem.at[3]))
        ref = place(yn(2), z, *part_a)
        send(ref, ref, az_sem.at[yn(2), 1], dev(x, c, y, zn(1)), is_owner)
        send(ref, ref, az_sem.at[yn(2), NZ - 1], dev(x, c, y, zn(-1)), is_owner)

    def ev_az(step, offset):
        cond = member(step)
        src_y = yn(offset)
        sems = lambda i: az_sem.at[src_y, i]
        when(cond, lambda: z_arrived(step, src_y, part_a, sems))
        z_forward(step, src_y, part_a, sems, cond)

    ev_ay()
    for step in (1, -1):
        ev_bz(step)
    ev_ayend()
    ev_by(0)
    for step in (1, -1):
        for offset in (0, 1, -1):
            ev_az(step, offset)
    for step in (2, -2):
        ev_bz(step)
    for step in (1, -1):
        ev_az(step, 2)
        ev_by(step)
    for step in (2, -2):
        for offset in (0, 1, -1):
            ev_az(step, offset)
    for step in (3, -3):
        ev_bz(step)
    for step in (2, -2):
        ev_az(step, 2)
        ev_by(step)
    for step in (3, -3):
        for offset in (0, 1, -1, 2):
            ev_az(step, offset)
        ev_by(step)
    ev_bz(4)
    for offset in (0, 1, -1, 2):
        ev_az(4, offset)
    ev_by(4)
    for step in (0, 1, -1, 2, -2, 3, -3, 4):
        ev_byend(step)
    drain(pending)
    pl.when(is_owner)(
        pltpu.make_async_copy(fin, place(y, z, 0, block_rows), load_sem.at[0]).wait
    )


def on_device(tokens, pre_act, act_grad):
    tok, feat = tokens.shape
    width = pre_act.shape[1]
    feats, cols = feat // 2, width // 2
    rows = feats * NX
    bf16, f32 = jnp.bfloat16, jnp.float32
    dma = pltpu.SemaphoreType.DMA
    return pl.pallas_call(
        kernel,
        out_shape=jax.ShapeDtypeStruct((feat * 2 * NX, width), bf16),
        in_specs=[
            pl.BlockSpec(memory_space=pltpu.VMEM),
            pl.BlockSpec(memory_space=pl.ANY),
            pl.BlockSpec(memory_space=pl.ANY),
        ],
        out_specs=pl.BlockSpec(memory_space=pl.ANY),
        scratch_shapes=[
            pltpu.VMEM((NZ, NX, feats, tok), bf16),
            pltpu.VMEM((NZ, tok, cols), bf16),
            pltpu.VMEM((2, tok, cols), bf16),
            pltpu.VMEM((tok, width), bf16),
            pltpu.VMEM((tok, width), bf16),
            pltpu.VMEM((NZ, rows, cols), bf16),
            pltpu.VMEM((256, 256), f32),
            pltpu.VMEM((NY, feats, cols), bf16),
            pltpu.VMEM((NY, 2 * feats, cols), bf16),
            pltpu.VMEM((2 * feats, cols), bf16),
            pltpu.VMEM((2 * NX, 8, 128), f32),
            pltpu.VMEM((NZ, 8, 128), f32),
            pltpu.VMEM((NX * NY, 8, 128), f32),
            pltpu.VMEM((NZ, 8, 128), f32),
            dma((2,)),
            dma((SEND_SEMS,)),
            dma((NZ,)),
            dma((NZ, 4)),
            dma((NZ,)),
            dma((NZ,)),
            dma((NY, 2)),
            dma((4,)),
            dma((NZ,)),
            dma((NZ, 4)),
            dma((NY, NZ)),
            dma((4,)),
        ],
        compiler_params=pltpu.CompilerParams(
            collective_id=0, has_side_effects=True, vmem_limit_bytes=48 * 1024 * 1024
        ),
    )(tokens.T, pre_act, act_grad)


def solution(mesh):
    return jax.shard_map(
        on_device,
        mesh=mesh,
        in_specs=(P("dp", "tp"), P("dp", "tp"), P("dp", "tp")),
        out_specs=P(None, "tp"),
        check_vma=False,
    )
```

```python
import jax
import jax.numpy as jnp
from jax import lax
from jax.experimental import pallas as pl
from jax.experimental.pallas import tpu as pltpu
from jax.sharding import PartitionSpec as P

norm_epsilon = 1e-06
gelu_scale = 0.7978845608
MESH = pl.DeviceIdType.MESH
NX, NY, NZ = 4, 4, 8
SEND_SEMS = 192


def gelu_slope(values):
    inner = gelu_scale * (values + 0.044715 * values * values * values)
    tangent = jnp.tanh(inner)
    return 0.5 * (1.0 + tangent) + 0.5 * values * (1.0 - tangent * tangent) * gelu_scale * (
        1.0 + 0.134145 * values * values
    )


def signed(step):
    return step if step <= NZ // 2 else step - NZ


def tree_weights(gram, strides):
    shape = gram.shape
    row = lax.broadcasted_iota(jnp.int32, shape, 0)
    lane = lax.broadcasted_iota(jnp.int32, shape, 1)
    own = lane % 8 == row
    first = lane < 8
    weight = jnp.ones((8, 1), jnp.float32)
    for stride in strides:
        pair = lane % 8 == (row + stride) % 8
        own_col = jnp.sum(jnp.where(own & first, gram, 0.0), axis=1, keepdims=True)
        pair_col = jnp.sum(jnp.where(pair & first, gram, 0.0), axis=1, keepdims=True)
        own_row = jnp.sum(jnp.where(own, gram, 0.0), axis=0, keepdims=True)
        pair_row = jnp.sum(
            jnp.where(row == (lane + stride) % 8, gram, 0.0), axis=0, keepdims=True
        )
        coef_col = 1.0 - pair_col / (2.0 * (jnp.maximum(own_col, 0.0) + norm_epsilon))
        coef_row = 1.0 - pair_row / (2.0 * (jnp.maximum(own_row, 0.0) + norm_epsilon))
        weight = weight * coef_col
        scaled = gram * coef_col * coef_row
        scaled = scaled + pltpu.roll(scaled, stride, 0)
        gram = scaled + pltpu.roll(scaled, stride, 1)
    return weight


def lane_sums(values):
    total = values[:, :128]
    for start in range(128, values.shape[1], 128):
        total = total + values[:, start:start + 128]
    return total[:8] + total[8:]


def exact_dot(left, right):
    return jnp.dot(
        left, right, preferred_element_type=jnp.float32, precision=lax.Precision.HIGHEST
    )


def fold(sums):
    size = sums.shape[0] * sums.shape[1] * sums.shape[2]
    across = exact_dot(sums.reshape(size, 128), jnp.ones((128, 128), jnp.float32))
    row = lax.broadcasted_iota(jnp.int32, (size, 128), 0)
    lane = lax.broadcasted_iota(jnp.int32, (size, 128), 1)
    kept = jnp.where(row // 8 % 8 == lane % 8, across, 0.0)
    return jnp.sum(kept.reshape(8, size // 8, 128), axis=1)


def kernel(
    xt, pre, act, out,
    xb, yb, ys, pre_v, act_v, grads, pairs, vs, vr, fin,
    a1, a2, b1, b2,
    load_sem, send_sem, xz_sem, xx_sem, yz_sem, yy_sem, v_sem, ar_sem,
    bz_sem, by_sem, az_sem, ay_sem,
):
    dp, tp = lax.axis_index("dp"), lax.axis_index("tp")
    z, y, x, c = dp // NY, dp % NY, tp // 2, tp % 2
    toward = 1 - 2 * (z % 2)
    kind = (z + 1) // 2 % 2
    tokens = yb.shape[1]
    half_tok = tokens // 2
    feats = xb.shape[2]
    cols = yb.shape[2]

    def dev(x_, c_, y_, z_):
        return (z_ * NY + y_, x_ * 2 + c_)

    def zn(step):
        return (z + step + NZ) % NZ

    def zt(step):
        return zn(step * toward)

    def yn(step):
        return (y + step + NY) % NY

    def xn(step):
        return (x + step + NX) % NX

    pending = []
    counter = [0]

    def send(src, dst, recv, device, cond=None, size=None):
        copy = pltpu.make_async_remote_copy(
            src_ref=src, dst_ref=dst, send_sem=send_sem.at[counter[0]], recv_sem=recv,
            device_id=device, device_id_type=MESH,
        )
        if cond is None:
            copy.start()
        else:
            pl.when(cond)(copy.start)
        pending.append((size or (lambda: src), counter[0], cond))
        counter[0] += 1

    def arrived(ref, sem):
        pltpu.make_async_copy(ref, ref, sem).wait()

    def drain(items):
        for ref, index, cond in items:
            if cond is None:
                arrived(ref(), send_sem.at[index])
            else:
                pl.when(cond)(lambda: arrived(ref(), send_sem.at[index]))

    loads = [
        pltpu.make_async_copy(pre, pre_v, load_sem.at[0]),
        pltpu.make_async_copy(act, act_v, load_sem.at[1]),
    ]
    for load in loads:
        load.start()

    barrier = pltpu.get_barrier_semaphore()
    partners = [dev(x, k, y, zn(s)) for s in range(1, NZ) for k in range(2)]
    partners += [dev(x, 1 - c, y, z)]
    partners += [dev(xn(s), k, y, z) for s in range(1, NX) for k in range(2)]
    partners += [dev(x, k, yn(s), z) for s in range(1, NY) for k in range(2)]
    partners += [dev(xn(s), c, yn(t), z) for s in range(1, NX) for t in range(1, NY)]
    for partner in partners:
        pl.semaphore_signal(barrier, inc=1, device_id=partner, device_id_type=MESH)
    pl.semaphore_wait(barrier, len(partners))

    match = kind == c
    for near, far in ((-1, 3), (1, -2)):
        cond = match if near < 0 else jnp.logical_not(match)
        for k in range(2):
            rows = xt.at[pl.ds(k * feats, feats)]
            send(rows, xb.at[z, x], xz_sem.at[z], dev(x, k, y, zt(far)), cond)
            send(rows, xb.at[z, x], xz_sem.at[z], dev(x, k, y, zt(near)), cond)
    other = pl.multiple_of((1 - c) * feats, 16)
    mine = pl.multiple_of(c * feats, 16)
    own_x = pltpu.make_async_copy(xt.at[pl.ds(mine, feats)], xb.at[z, x], xz_sem.at[z])
    pl.when(match)(own_x.start)
    send(xt.at[pl.ds(other, feats)], xb.at[z, x], xz_sem.at[z], dev(x, 1 - c, y, z), match)

    chunk = 32
    my_pair, my_parity = z // 2, z % 2
    first = jnp.where((c - my_pair + 4) % 4 == 0, 1, 0)

    def ev_sl(turn):
        if turn == 0:
            for load in loads:
                load.wait()
        j = first if turn == 0 else 1 - first
        span = pl.ds(pl.multiple_of(j * cols, 128), cols)

        def slope_rows(i, carry):
            rows = pl.ds(pl.multiple_of(i * chunk, chunk), chunk)
            slope = gelu_slope(pre_v[rows, span].astype(jnp.float32))
            ys[turn, rows, :] = (act_v[rows, span].astype(jnp.float32) * slope).astype(jnp.bfloat16)
            return carry

        lax.fori_loop(0, tokens // chunk, slope_rows, 0)

    def ev_ys(turn):
        pair = c + 2 * (first if turn == 0 else 1 - first)
        ahead = (pair - my_pair + 4) % 4
        upper = jnp.where(
            ahead == 0, 1 - my_parity,
            jnp.where(ahead == 3, 1, jnp.where(ahead == 2, 1 - my_parity, 0)),
        )
        target = 2 * pair + upper
        for k in range(2):
            rows = pl.ds(k * half_tok, half_tok)
            send(ys.at[turn, rows], yb.at[z, rows], yz_sem.at[z], dev(x, k, y, target))
        own = ahead == 0
        own_rows = pl.ds(pl.multiple_of(c * half_tok, 16), half_tok)
        other_rows = pl.ds(pl.multiple_of((1 - c) * half_tok, 16), half_tok)
        own_y = pltpu.make_async_copy(ys.at[turn, own_rows], yb.at[z, own_rows], yz_sem.at[z])
        pl.when(own)(own_y.start)
        send(ys.at[turn, other_rows], yb.at[z, other_rows], yz_sem.at[z], dev(x, 1 - c, y, z), own)

    def ev_xz(step):
        src = zt(step)
        piece = xb.at[src, x]
        arrived(piece, xz_sem.at[src])
        if step in (1, 2, 3):
            send(piece, piece, xz_sem.at[src], dev(x, c, y, zt(-1)))
        send(piece, piece, xx_sem.at[src, 0], dev(xn(1), c, y, z))
        send(piece, piece, xx_sem.at[src, 1], dev(xn(-1), c, y, z))

    low, high = pl.ds(0, feats // 2), pl.ds(feats // 2, feats // 2)

    def ev_xx(step):
        src = zt(step)
        left, right = xb.at[src, xn(-1)], xb.at[src, xn(1)]
        arrived(left, xx_sem.at[src, 0])
        send(left.at[low], left.at[low], xx_sem.at[src, 2], dev(xn(1), c, y, z))
        arrived(right, xx_sem.at[src, 1])
        send(right.at[high], right.at[high], xx_sem.at[src, 3], dev(xn(-1), c, y, z))

    my_tok = pl.ds(pl.multiple_of(c * half_tok, 16), half_tok)
    its_tok = pl.ds(pl.multiple_of((1 - c) * half_tok, 16), half_tok)

    def ev_yz(step):
        src = zt(step)
        piece = yb.at[src, my_tok]
        arrived(piece, yz_sem.at[src])
        if step in (-1, -2, -3):
            send(piece, piece, yz_sem.at[src], dev(x, c, y, zt(1)))
        send(piece, piece, yy_sem.at[src], dev(x, 1 - c, y, z))

    def ev_mm(step):
        src = zt(step)
        far = xb.at[src, xn(2)]
        arrived(far.at[low], xx_sem.at[src, 2])
        arrived(far.at[high], xx_sem.at[src, 3])
        arrived(yb.at[src, its_tok], yy_sem.at[src])

        def block(i, carry):
            result = jnp.dot(xb[src, i], yb[src], preferred_element_type=jnp.float32)
            grads[src, pl.ds(pl.multiple_of(i * feats, 16), feats), :] = result.astype(jnp.bfloat16)
            return carry

        lax.fori_loop(0, NX, block, 0)
        done.append(src)

        def products(i, sums):
            rows = pl.ds(pl.multiple_of(i * 16, 16), 16)
            new = grads[src, rows, :].astype(jnp.float32)
            return tuple(
                total + lane_sums(new * (new if old is src else grads[old, rows, :].astype(jnp.float32)))
                for old, total in zip(done, sums)
            )

        zero = jnp.zeros((8, 128), jnp.float32)
        sums = lax.fori_loop(0, grads.shape[1] // 16, products, (zero,) * len(done))
        for old, total in zip(done, sums):
            pairs[src, old] = total
            if old is not src:
                pairs[old, src] = total

    done = []
    xz, xx, yz, mm = ev_xz, ev_xx, ev_yz, ev_mm
    sl, yt = ev_sl, ev_ys
    for event, step in [
        (xz, 0), (sl, 0), (xz, -1), (xz, 1), (sl, 1), (xx, 0), (xz, 2), (xz, 3), (yt, 0), (yt, 1),
        (xx, -1), (xx, 1), (xz, -2), (xz, -3), (xx, 2), (xz, 4), (yz, 0), (yz, 1), (yz, -1), (xx, 3), (xx, -2), (xx, -3),
        (mm, 0), (yz, -2), (xx, 4), (mm, 1), (yz, -3), (mm, -1), (yz, 2), (mm, -2), (yz, 3),
        (mm, 2), (mm, -3), (yz, 4), (mm, 3), (mm, 4),
    ]:
        event(step)

    out_lane = lax.broadcasted_iota(jnp.int32, (8, 128), 1)
    a1[tp] = fold(pairs[...])
    for s in range(1, 2 * NX):
        send(a1.at[tp], a1.at[tp], ar_sem.at[0], (dp, (tp + s) % (2 * NX)))
    sent = pl.ds(0, 2 * NX - 1)
    arrived(a1.at[sent], ar_sem.at[0])
    a2[z] = jnp.sum(a1[...], axis=0)
    for s in range(1, NZ):
        send(a2.at[z], a2.at[z], ar_sem.at[1], dev(x, c, y, zn(s)))
    arrived(a2.at[pl.ds(0, NZ - 1)], ar_sem.at[1])
    weight = tree_weights(jnp.sum(a2[...], axis=0), (4, 2, 1))

    owner = z // 2 % 2
    is_owner = c == owner
    its_rows = pl.ds(pl.multiple_of(c * feats, 16), feats)
    small = 32
    for s in (1, -1, 2, 0):
        part = yn(s)

        def combine_rows(i, carry):
            total = jnp.zeros((small, cols), jnp.float32)
            rows = pl.ds(pl.multiple_of(part * feats + i * small, 32), small)
            for r in range(NZ):
                total += weight[r:r + 1, :] * grads[r, rows, :].astype(jnp.float32)
            vs[part, pl.ds(pl.multiple_of(i * small, small), small), :] = total.astype(jnp.bfloat16)
            return carry

        lax.fori_loop(0, feats // small, combine_rows, 0)
        if s:
            send(vs.at[part], vr.at[y, its_rows], v_sem.at[y, c], dev(x, owner, part, z))
        else:
            own_v = pltpu.make_async_copy(vs.at[part], vr.at[y, its_rows], v_sem.at[y, c])
            pl.when(is_owner)(own_v.start)
            send(vs.at[part], vr.at[y, its_rows], v_sem.at[y, c], dev(x, owner, part, z),
                 jnp.logical_not(is_owner))

    block_rows = 2 * feats
    cut = block_rows * 2 // 5
    part_a, part_b = (0, cut), (cut, block_rows - cut)

    def place(y_, z_, start, size):
        top = pl.multiple_of((2 * y_ + (z_ + 1) // 2 % 2) * block_rows + start, 16)
        left = pl.multiple_of(z_ // 4 * cols, 128)
        return out.at[pl.ds(top, size), pl.ds(left, cols)]

    def halves(part):
        start, size = part
        return (start, size // 2), (start + size // 2, size // 2)

    def finish():
        for src in range(NY):
            for k in range(2):
                arrived(vr.at[src, pl.ds(k * feats, feats)], v_sem.at[src, k])
        def products(i, sums):
            rows = pl.ds(pl.multiple_of(i * 16, 16), 16)
            parts = [vr[r, rows, :].astype(jnp.float32) for r in range(NY)]
            return tuple(
                total + lane_sums(parts[a] * parts[b]) for (a, b), total in zip(combos, sums)
            )

        combos = [(a, b) for a in range(NY) for b in range(a, NY)]
        zero = jnp.zeros((8, 128), jnp.float32)
        sums = lax.fori_loop(0, block_rows // 16, products, (zero,) * len(combos))
        out_row = lax.broadcasted_iota(jnp.int32, (8, 128), 0) % NY
        out_col = out_lane % NY
        gram = zero
        for (a, b), total in zip(combos, sums):
            value = jnp.sum(total, axis=(0, 1), keepdims=True)
            spot = ((out_row == a) & (out_col == b)) | ((out_row == b) & (out_col == a))
            gram = jnp.where(spot, value, gram)
        me = x * NY + y
        b1[me] = gram
        for s in range(NX):
            for t in range(NY):
                if s or t:
                    send(b1.at[me], b1.at[me], ar_sem.at[2], dev(xn(s), c, yn(t), z), size=lambda: b1.at[0])
        arrived(b1.at[pl.ds(0, NX * NY - 1)], ar_sem.at[2])
        b2[z] = jnp.sum(b1[...], axis=0)
        for s in range(1, NZ):
            send(b2.at[z], b2.at[z], ar_sem.at[3], dev(x, zn(s) // 2 % 2, y, zn(s)), size=lambda: b2.at[0])
        arrived(b2.at[pl.ds(0, NZ - 1)], ar_sem.at[3])
        last = tree_weights(jnp.sum(b2[...], axis=0), (2, 1))

        def final_rows(i, carry):
            total = jnp.zeros((small, cols), jnp.float32)
            rows = pl.ds(pl.multiple_of(i * small, small), small)
            for r in range(NY):
                total += last[r:r + 1, :] * vr[r, rows, :].astype(jnp.float32)
            fin[rows, :] = total.astype(jnp.bfloat16)
            return carry

        lax.fori_loop(0, block_rows // small, final_rows, 0)
        def launch(part, sem, device):
            send(fin.at[pl.ds(*part)], place(y, z, *part), sem, device,
                 size=lambda: fin.at[pl.ds(*part)])

        for s in (1, -1):
            launch(part_b, bz_sem.at[s % NZ], dev(x, c, y, zn(s)))
            launch(part_a, ay_sem.at[0 if s > 0 else 1], dev(x, c, yn(s), z))
        for s in (1, -1):
            launch(part_b, by_sem.at[0, 0 if s > 0 else 1], dev(x, c, yn(s), z))
            launch(part_a, az_sem.at[y, s % NZ], dev(x, c, y, zn(s)))
        pltpu.make_async_copy(fin, place(y, z, 0, block_rows), load_sem.at[0]).start()

    mark = len(pending)
    pl.when(is_owner)(finish)
    pending[mark:] = [(ref, index, is_owner) for ref, index, _ in pending[mark:]]

    def z_forward(step, src_y, part, sems, cond):
        src = zn(-step)
        first, second = halves(part)
        if step in (1, 2):
            ref = place(src_y, src, *part)
            send(ref, ref, sems(step + 1), dev(x, c, y, zn(1)), cond)
        elif step in (-1, -2):
            ref = place(src_y, src, *part)
            send(ref, ref, sems((step - 1) % NZ), dev(x, c, y, zn(-1)), cond)
        elif step == 3:
            ref = place(src_y, src, *first)
            send(ref, ref, sems(4), dev(x, c, y, zn(1)), cond)
        elif step == -3:
            ref = place(src_y, src, *second)
            send(ref, ref, sems(0), dev(x, c, y, zn(-1)), cond)

    def z_arrived(step, src_y, part, sems):
        src = zn(-step)
        first, second = halves(part)
        if step == 4:
            arrived(place(src_y, src, *first), sems(4))
            arrived(place(src_y, src, *second), sems(0))
        else:
            arrived(place(src_y, src, *part), sems(step % NZ))

    def member(step):
        return zn(-step) // 2 % 2 == c

    def when(cond, task):
        pl.when(cond)(task)

    def ev_bz(step):
        cond = member(step)
        when(cond, lambda: z_arrived(step, y, part_b, lambda i: bz_sem.at[i]))
        z_forward(step, y, part_b, lambda i: bz_sem.at[i], cond)
        ref = place(y, zn(-step), *part_b)
        send(ref, ref, by_sem.at[step % NZ, 0], dev(x, c, yn(1), z), cond)
        send(ref, ref, by_sem.at[step % NZ, 1], dev(x, c, yn(-1), z), cond)

    def spread_y(sem, part, src_z, cond):
        first, second = halves(part)
        left, right = place(yn(-1), src_z, *part), place(yn(1), src_z, *part)
        when(cond, lambda: arrived(left, sem(0)))
        ref = place(yn(-1), src_z, *first)
        send(ref, ref, sem(2), dev(x, c, yn(1), z), cond)
        when(cond, lambda: arrived(right, sem(1)))
        ref = place(yn(1), src_z, *second)
        send(ref, ref, sem(3), dev(x, c, yn(-1), z), cond)

    def ev_by(step):
        spread_y(lambda i: by_sem.at[step % NZ, i], part_b, zn(-step), member(step))

    def ev_byend(step):
        first, second = halves(part_b)
        cond = member(step)
        when(cond, lambda: arrived(place(yn(2), zn(-step), *first), by_sem.at[step % NZ, 2]))
        when(cond, lambda: arrived(place(yn(2), zn(-step), *second), by_sem.at[step % NZ, 3]))

    def ev_ay():
        spread_y(lambda i: ay_sem.at[i], part_a, z, is_owner)
        for s in (1, -1):
            ref = place(yn(-s), z, *part_a)
            send(ref, ref, az_sem.at[yn(-s), 1], dev(x, c, y, zn(1)), is_owner)
            send(ref, ref, az_sem.at[yn(-s), NZ - 1], dev(x, c, y, zn(-1)), is_owner)

    def ev_ayend():
        first, second = halves(part_a)
        when(is_owner, lambda: arrived(place(yn(2), z, *first), ay_sem.at[2]))
        when(is_owner, lambda: arrived(place(yn(2), z, *second), ay_sem.at[3]))
        ref = place(yn(2), z, *part_a)
        send(ref, ref, az_sem.at[yn(2), 1], dev(x, c, y, zn(1)), is_owner)
        send(ref, ref, az_sem.at[yn(2), NZ - 1], dev(x, c, y, zn(-1)), is_owner)

    def ev_az(step, offset):
        cond = member(step)
        src_y = yn(offset)
        sems = lambda i: az_sem.at[src_y, i]
        when(cond, lambda: z_arrived(step, src_y, part_a, sems))
        z_forward(step, src_y, part_a, sems, cond)

    ev_ay()
    for step in (1, -1):
        ev_bz(step)
    ev_ayend()
    ev_by(0)
    for step in (1, -1):
        for offset in (0, 1, -1):
            ev_az(step, offset)
    for step in (2, -2):
        ev_bz(step)
    for step in (1, -1):
        ev_az(step, 2)
        ev_by(step)
    for step in (2, -2):
        for offset in (0, 1, -1):
            ev_az(step, offset)
    for step in (3, -3):
        ev_bz(step)
    for step in (2, -2):
        ev_az(step, 2)
        ev_by(step)
    for step in (3, -3):
        for offset in (0, 1, -1, 2):
            ev_az(step, offset)
        ev_by(step)
    ev_bz(4)
    for offset in (0, 1, -1, 2):
        ev_az(4, offset)
    ev_by(4)
    for step in (0, 1, -1, 2, -2, 3, -3, 4):
        ev_byend(step)
    drain(pending)
    pl.when(is_owner)(
        pltpu.make_async_copy(fin, place(y, z, 0, block_rows), load_sem.at[0]).wait
    )


def on_device(tokens, pre_act, act_grad):
    tok, feat = tokens.shape
    width = pre_act.shape[1]
    feats, cols = feat // 2, width // 2
    rows = feats * NX
    bf16, f32 = jnp.bfloat16, jnp.float32
    dma = pltpu.SemaphoreType.DMA
    return pl.pallas_call(
        kernel,
        out_shape=pltpu.VMEM((feat * 2 * NX, width), bf16),
        in_specs=[
            pl.BlockSpec(memory_space=pl.ANY),
            pl.BlockSpec(memory_space=pl.ANY),
            pl.BlockSpec(memory_space=pl.ANY),
        ],
        out_specs=pl.BlockSpec(memory_space=pltpu.VMEM),
        scratch_shapes=[
            pltpu.VMEM((NZ, NX, feats, tok), bf16),
            pltpu.VMEM((NZ, tok, cols), bf16),
            pltpu.VMEM((2, tok, cols), bf16),
            pltpu.VMEM((tok, width), bf16),
            pltpu.VMEM((tok, width), bf16),
            pltpu.VMEM((NZ, rows, cols), bf16),
            pltpu.VMEM((NZ, NZ, 8, 128), f32),
            pltpu.VMEM((NY, feats, cols), bf16),
            pltpu.VMEM((NY, 2 * feats, cols), bf16),
            pltpu.VMEM((2 * feats, cols), bf16),
            pltpu.VMEM((2 * NX, 8, 128), f32),
            pltpu.VMEM((NZ, 8, 128), f32),
            pltpu.VMEM((NX * NY, 8, 128), f32),
            pltpu.VMEM((NZ, 8, 128), f32),
            dma((2,)),
            dma((SEND_SEMS,)),
            dma((NZ,)),
            dma((NZ, 4)),
            dma((NZ,)),
            dma((NZ,)),
            dma((NY, 2)),
            dma((4,)),
            dma((NZ,)),
            dma((NZ, 4)),
            dma((NY, NZ)),
            dma((4,)),
        ],
        compiler_params=pltpu.CompilerParams(
            collective_id=0, has_side_effects=True, vmem_limit_bytes=52 * 1024 * 1024
        ),
    )(tokens.T, pre_act, act_grad)


def solution(mesh):
    return jax.shard_map(
        on_device,
        mesh=mesh,
        in_specs=(P("dp", "tp"), P("dp", "tp"), P("dp", "tp")),
        out_specs=P(None, "tp"),
        check_vma=False,
    )
```

```python
import jax
import jax.numpy as jnp
from jax import lax
from jax.experimental import pallas as pl
from jax.experimental.pallas import tpu as pltpu
from jax.sharding import PartitionSpec as P

norm_epsilon = 1e-06
gelu_scale = 0.7978845608
MESH = pl.DeviceIdType.MESH
NX, NY, NZ = 4, 4, 8
SEND_SEMS = 80

OWNER_EVENTS = [
    ("source_y",), ("source_z",), ("first_z", 0), ("turn_y", 0), ("pass_y",), ("first_z", -1),
    ("b_along_z", -1), ("turn_y", -1), ("last_y",), ("first_z", 2), ("first_z", 1), ("b_along_y", 0),
    ("a_along_z", -1, 2), ("b_along_y", -1), ("a_along_z", -1, 0), ("a_along_z", -1, 1), ("b_along_z", 3),
    ("a_along_z", -1, -1), ("turn_y", 3), ("b_along_z", 4), ("b_end", -1), ("b_end", 0), ("turn_y", 4),
    ("a_along_z", 3, -1), ("a_along_z", 3, 2), ("b_along_y", 3), ("b_along_y", 4), ("a_along_z", 4, 0),
    ("a_along_z", 4, 1), ("a_along_z", 3, 1), ("a_along_z", 4, 2), ("b_end", 3), ("a_along_z", 3, 0),
    ("a_along_z", 4, -1), ("b_end", 4),
]
OTHER_EVENTS = [
    ("b_along_z", 1), ("turn_y", 1), ("b_along_z", -2), ("turn_y", -2), ("b_along_z", 2), ("turn_y", 2),
    ("a_along_z", 1, 2), ("a_along_z", 1, 1), ("a_along_z", 1, -1), ("a_along_z", 1, 0), ("a_along_z", 2, 0),
    ("b_along_z", -3), ("b_along_y", 1), ("turn_y", -3), ("a_along_z", -2, 1), ("a_along_z", -2, 2),
    ("b_along_y", 2), ("a_along_z", 2, -1), ("a_along_z", 2, 1), ("a_along_z", -2, -1), ("b_end", 1),
    ("a_along_z", 2, 2), ("a_along_z", -3, 0), ("b_along_y", -2), ("b_along_y", -3), ("a_along_z", -3, -1),
    ("a_along_z", -2, 0), ("a_along_z", -3, 1), ("a_along_z", -3, 2), ("b_end", 2), ("b_end", -3),
    ("b_end", -2),
]


def gelu_slope(values):
    inner = gelu_scale * (values + 0.044715 * values * values * values)
    tangent = jnp.tanh(inner)
    return 0.5 * (1.0 + tangent) + 0.5 * values * (1.0 - tangent * tangent) * gelu_scale * (
        1.0 + 0.134145 * values * values
    )


def tree_weights(gram, strides):
    shape = gram.shape
    row = lax.broadcasted_iota(jnp.int32, shape, 0)
    lane = lax.broadcasted_iota(jnp.int32, shape, 1)
    own = lane % 8 == row
    first = lane < 8
    weight = jnp.ones((8, 1), jnp.float32)
    for stride in strides:
        pair = lane % 8 == (row + stride) % 8
        own_col = jnp.sum(jnp.where(own & first, gram, 0.0), axis=1, keepdims=True)
        pair_col = jnp.sum(jnp.where(pair & first, gram, 0.0), axis=1, keepdims=True)
        own_row = jnp.sum(jnp.where(own, gram, 0.0), axis=0, keepdims=True)
        pair_row = jnp.sum(
            jnp.where(row == (lane + stride) % 8, gram, 0.0), axis=0, keepdims=True
        )
        coef_col = 1.0 - pair_col / (2.0 * (jnp.maximum(own_col, 0.0) + norm_epsilon))
        coef_row = 1.0 - pair_row / (2.0 * (jnp.maximum(own_row, 0.0) + norm_epsilon))
        weight = weight * coef_col
        scaled = gram * coef_col * coef_row
        scaled = scaled + pltpu.roll(scaled, stride, 0)
        gram = scaled + pltpu.roll(scaled, stride, 1)
    return weight


def lane_sums(values):
    total = values[:, :128]
    for start in range(128, values.shape[1], 128):
        total = total + values[:, start:start + 128]
    return total[:8] + total[8:]


def exact_dot(left, right):
    return jnp.dot(
        left, right, preferred_element_type=jnp.float32, precision=lax.Precision.HIGHEST
    )


def fold(sums):
    size = sums.shape[0] * sums.shape[1] * sums.shape[2]
    across = exact_dot(sums.reshape(size, 128), jnp.ones((128, 128), jnp.float32))
    row = lax.broadcasted_iota(jnp.int32, (size, 128), 0)
    lane = lax.broadcasted_iota(jnp.int32, (size, 128), 1)
    kept = jnp.where(row // 8 % 8 == lane % 8, across, 0.0)
    return jnp.sum(kept.reshape(8, size // 8, 128), axis=1)


def kernel(
    xt, pre, act, out,
    xb, yb, ys, pre_v, act_v, grads, pairs, vs, vr,
    a1, a2, b1, b2,
    load_sem, send_sem, group_sem, xz_sem, xx_sem, yz_sem, yy_sem, v_sem, ar_sem,
    bz_sem, by_sem, az_sem, ay_sem,
):
    dp, tp = lax.axis_index("dp"), lax.axis_index("tp")
    z, y, x, c = dp // NY, dp % NY, tp // 2, tp % 2
    toward = 1 - 2 * (z % 2)
    kind = (z + 1) // 2 % 2
    tokens = yb.shape[1]
    half_tok = tokens // 2
    feats = xb.shape[2]
    cols = yb.shape[2]

    def dev(x_, c_, y_, z_):
        return (z_ * NY + y_, x_ * 2 + c_)

    def zn(step):
        return (z + step + NZ) % NZ

    def zt(step):
        return zn(step * toward)

    def yn(step):
        return (y + step + NY) % NY

    def xn(step):
        return (x + step + NX) % NX

    pending = []
    counter = [0]

    def send(src, dst, recv, device, cond=None, group=None, waits=pending):
        if group is None:
            sent = send_sem.at[counter[0]]
            waits.append((src, counter[0], cond))
            counter[0] += 1
        else:
            sent = group_sem.at[group]
        copy = pltpu.make_async_remote_copy(
            src_ref=src, dst_ref=dst, send_sem=sent, recv_sem=recv,
            device_id=device, device_id_type=MESH,
        )
        if cond is None:
            copy.start()
        else:
            pl.when(cond)(copy.start)

    def arrived(ref, sem):
        pltpu.make_async_copy(ref, ref, sem).wait()

    def drain(items):
        for ref, index, cond in items:
            if cond is None:
                arrived(ref, send_sem.at[index])
            else:
                pl.when(cond)(lambda: arrived(ref, send_sem.at[index]))

    loads = [
        pltpu.make_async_copy(pre, pre_v, load_sem.at[0]),
        pltpu.make_async_copy(act, act_v, load_sem.at[1]),
    ]
    for load in loads:
        load.start()

    barrier = pltpu.get_barrier_semaphore()
    partners = [dev(x, k, y, zn(s)) for s in range(1, NZ) for k in range(2)]
    partners += [dev(x, 1 - c, y, z)]
    partners += [dev(xn(s), k, y, z) for s in range(1, NX) for k in range(2)]
    partners += [dev(x, k, yn(s), z) for s in range(1, NY) for k in range(2)]
    partners += [dev(xn(s), c, yn(t), z) for s in range(1, NX) for t in range(1, NY)]
    for partner in partners:
        pl.semaphore_signal(barrier, inc=1, device_id=partner, device_id_type=MESH)
    pl.semaphore_wait(barrier, len(partners))

    match = kind == c
    for near, far in ((-1, 3), (1, -2)):
        cond = match if near < 0 else jnp.logical_not(match)
        for k in range(2):
            rows = xt.at[pl.ds(k * feats, feats)]
            send(rows, xb.at[z, x], xz_sem.at[z], dev(x, k, y, zt(far)), cond, group=0)
            send(rows, xb.at[z, x], xz_sem.at[z], dev(x, k, y, zt(near)), cond, group=0)
    other = pl.multiple_of((1 - c) * feats, 16)
    mine = pl.multiple_of(c * feats, 16)
    own_x = pltpu.make_async_copy(xt.at[pl.ds(mine, feats)], xb.at[z, x], xz_sem.at[z])
    pl.when(match)(own_x.start)
    send(xt.at[pl.ds(other, feats)], xb.at[z, x], xz_sem.at[z], dev(x, 1 - c, y, z), match)

    chunk = 32
    my_pair, my_parity = z // 2, z % 2
    first = jnp.where((c - my_pair + 4) % 4 == 0, 1, 0)

    def ev_sl(turn):
        if turn == 0:
            for load in loads:
                load.wait()
        j = first if turn == 0 else 1 - first
        span = pl.ds(pl.multiple_of(j * cols, 128), cols)

        def slope_rows(i, carry):
            rows = pl.ds(pl.multiple_of(i * chunk, chunk), chunk)
            slope = gelu_slope(pre_v[rows, span].astype(jnp.float32))
            ys[turn, rows, :] = (act_v[rows, span].astype(jnp.float32) * slope).astype(jnp.bfloat16)
            return carry

        lax.fori_loop(0, tokens // chunk, slope_rows, 0)

    def ev_ys(turn):
        pair = c + 2 * (first if turn == 0 else 1 - first)
        ahead = (pair - my_pair + 4) % 4
        upper = jnp.where(
            ahead == 0, 1 - my_parity,
            jnp.where(ahead == 3, 1, jnp.where(ahead == 2, 1 - my_parity, 0)),
        )
        target = 2 * pair + upper
        for k in range(2):
            rows = pl.ds(k * half_tok, half_tok)
            send(ys.at[turn, rows], yb.at[z, rows], yz_sem.at[z], dev(x, k, y, target), group=2)
        own = ahead == 0
        own_rows = pl.ds(pl.multiple_of(c * half_tok, 16), half_tok)
        other_rows = pl.ds(pl.multiple_of((1 - c) * half_tok, 16), half_tok)
        own_y = pltpu.make_async_copy(ys.at[turn, own_rows], yb.at[z, own_rows], yz_sem.at[z])
        pl.when(own)(own_y.start)
        send(ys.at[turn, other_rows], yb.at[z, other_rows], yz_sem.at[z], dev(x, 1 - c, y, z), own)

    def ev_xz(step):
        src = zt(step)
        piece = xb.at[src, x]
        arrived(piece, xz_sem.at[src])
        if step in (1, 2, 3):
            send(piece, piece, xz_sem.at[src], dev(x, c, y, zt(-1)), group=1)
        send(piece, piece, xx_sem.at[src, 0], dev(xn(1), c, y, z), group=0)
        send(piece, piece, xx_sem.at[src, 1], dev(xn(-1), c, y, z), group=0)

    low, high = pl.ds(0, feats // 2), pl.ds(feats // 2, feats // 2)

    def ev_xx(step):
        src = zt(step)
        left, right = xb.at[src, xn(-1)], xb.at[src, xn(1)]
        arrived(left, xx_sem.at[src, 0])
        send(left.at[low], left.at[low], xx_sem.at[src, 2], dev(xn(1), c, y, z), group=0)
        arrived(right, xx_sem.at[src, 1])
        send(right.at[high], right.at[high], xx_sem.at[src, 3], dev(xn(-1), c, y, z), group=0)

    my_tok = pl.ds(pl.multiple_of(c * half_tok, 16), half_tok)
    its_tok = pl.ds(pl.multiple_of((1 - c) * half_tok, 16), half_tok)

    def ev_yz(step):
        src = zt(step)
        piece = yb.at[src, my_tok]
        arrived(piece, yz_sem.at[src])
        if step in (-1, -2, -3):
            send(piece, piece, yz_sem.at[src], dev(x, c, y, zt(1)), group=3 if step == -3 else 2)
        send(piece, piece, yy_sem.at[src], dev(x, 1 - c, y, z), group=2)

    def ev_mm(step):
        src = zt(step)
        far = xb.at[src, xn(2)]
        arrived(far.at[low], xx_sem.at[src, 2])
        arrived(far.at[high], xx_sem.at[src, 3])
        arrived(yb.at[src, its_tok], yy_sem.at[src])

        def block(i, carry):
            result = jnp.dot(xb[src, i], yb[src], preferred_element_type=jnp.float32)
            grads[src, pl.ds(pl.multiple_of(i * feats, 16), feats), :] = result.astype(jnp.bfloat16)
            return carry

        lax.fori_loop(0, NX, block, 0)
        done.append(src)

        def products(i, sums):
            rows = pl.ds(pl.multiple_of(i * 16, 16), 16)
            new = grads[src, rows, :].astype(jnp.float32)
            return tuple(
                total + lane_sums(new * (new if old is src else grads[old, rows, :].astype(jnp.float32)))
                for old, total in zip(done, sums)
            )

        zero = jnp.zeros((8, 128), jnp.float32)
        sums = lax.fori_loop(0, grads.shape[1] // 16, products, (zero,) * len(done))
        for old, total in zip(done, sums):
            pairs[src, old] = total
            if old is not src:
                pairs[old, src] = total

    done = []
    xz, xx, yz, mm = ev_xz, ev_xx, ev_yz, ev_mm
    sl, yt = ev_sl, ev_ys
    for event, step in [
        (xz, 0), (sl, 0), (xz, -1), (xz, 1), (sl, 1), (xx, 0), (xz, 2), (xz, 3), (yt, 0), (yt, 1),
        (xx, -1), (xx, 1), (xz, -2), (xz, -3), (xx, 2), (xz, 4), (yz, 0), (yz, 1), (yz, -1), (xx, 3), (xx, -2), (xx, -3),
        (mm, 0), (yz, -2), (xx, 4), (mm, 1), (yz, -3), (mm, -1), (yz, 2), (mm, -2), (yz, 3),
        (mm, 2), (mm, -3), (yz, 4), (mm, 3), (mm, 4),
    ]:
        event(step)

    out_lane = lax.broadcasted_iota(jnp.int32, (8, 128), 1)
    a1[tp] = fold(pairs[...])
    for s in range(1, 2 * NX):
        send(a1.at[tp], a1.at[tp], ar_sem.at[0], (dp, (tp + s) % (2 * NX)), group=4)
    arrived(xb.at[pl.ds(0, 7)], group_sem.at[0])
    arrived(xb.at[0, pl.ds(0, 3)], group_sem.at[1])
    arrived(yb.at[pl.ds(0, 7)], group_sem.at[2])
    arrived(yb.at[0, pl.ds(0, half_tok)], group_sem.at[3])
    drain(pending)
    pending.clear()
    sent = pl.ds(0, 2 * NX - 1)
    arrived(a1.at[sent], ar_sem.at[0])
    a2[z] = jnp.sum(a1[...], axis=0)
    for s in range(1, NZ):
        send(a2.at[z], a2.at[z], ar_sem.at[1], dev(x, c, y, zn(s)), group=5)
    arrived(a1.at[sent], group_sem.at[4])
    arrived(a2.at[pl.ds(0, NZ - 1)], ar_sem.at[1])
    weight = tree_weights(jnp.sum(a2[...], axis=0), (4, 2, 1))

    owner = z // 2 % 2
    is_owner = c == owner
    its_rows = pl.ds(pl.multiple_of(c * feats, 16), feats)
    small = 32
    for s in (1, -1, 2, 0):
        part = yn(s)

        def combine_rows(i, carry):
            total = jnp.zeros((small, cols), jnp.float32)
            rows = pl.ds(pl.multiple_of(part * feats + i * small, 32), small)
            for r in range(NZ):
                total += weight[r:r + 1, :] * grads[r, rows, :].astype(jnp.float32)
            vs[part, pl.ds(pl.multiple_of(i * small, small), small), :] = total.astype(jnp.bfloat16)
            return carry

        lax.fori_loop(0, feats // small, combine_rows, 0)
        if s:
            send(vs.at[part], vr.at[y, its_rows], v_sem.at[y, c], dev(x, owner, part, z), group=6)
        else:
            own_v = pltpu.make_async_copy(vs.at[part], vr.at[y, its_rows], v_sem.at[y, c])
            pl.when(is_owner)(own_v.start)
            last_push = counter[0]
            send(vs.at[part], vr.at[y, its_rows], v_sem.at[y, c], dev(x, owner, part, z),
                 jnp.logical_not(is_owner))
            pending.clear()

    def settle():
        arrived(a2.at[pl.ds(0, NZ - 1)], group_sem.at[5])
        arrived(vs.at[pl.ds(0, NY - 1)], group_sem.at[6])

    block = 2 * feats
    cut = block * 2 // 5
    rest = block - cut

    def kind_of(z_):
        return (z_ + 1) // 2 % 2

    def span_of(n):
        return pl.ds(pl.multiple_of(n * cols, 128), cols)

    def part_a(y_, src, start=0, size=cut):
        return out.at[y_, kind_of(src), pl.ds(start, size), span_of(src // 4)]

    def part_b(y_, src):
        return out.at[y_, kind_of(src), pl.ds(cut, rest), span_of(src // 4)]

    class Gather:
        def __init__(self):
            self.waits = []

        def run(self, events):
            for name, *args in events:
                getattr(self, name)(*args)
            drain(self.waits)

        def go(self, ref, sem, device):
            send(ref, ref, sem, device, waits=self.waits)

        def source_z(self):
            for s in (1, -1):
                self.go(part_b(y, z), bz_sem.at[-s % NZ], dev(x, c, y, zt(s)))

        def source_y(self):
            for s in (1, -1):
                self.go(part_a(y, z), ay_sem.at[0 if s > 0 else 1], dev(x, c, yn(s), z))

        def pass_y(self):
            half = cut // 2
            arrived(part_a(yn(-1), z), ay_sem.at[0])
            self.go(part_a(yn(-1), z, 0, half), ay_sem.at[2], dev(x, c, yn(1), z))
            arrived(part_a(yn(1), z), ay_sem.at[1])
            self.go(part_a(yn(1), z, half, half), ay_sem.at[3], dev(x, c, yn(-1), z))

        def last_y(self):
            half = cut // 2
            arrived(part_a(yn(2), z, 0, half), ay_sem.at[2])
            arrived(part_a(yn(2), z, half, half), ay_sem.at[3])

        def first_z(self, offset):
            for s in (1, -1):
                self.go(part_a(yn(offset), z), az_sem.at[-s % NZ, offset % NY], dev(x, c, y, zt(s)))

        def along_z(self, ref, step, sem_at, opposite):
            arrived(ref, sem_at(step % NZ))
            sign = 1 if step > 0 else -1
            if abs(step) < 3 or (abs(step) == 3 and sign == opposite):
                self.go(ref, sem_at(-(step + sign) % NZ), dev(x, c, y, zt(sign)))

        def b_along_z(self, step):
            self.along_z(part_b(y, zt(-step)), step, lambda i: bz_sem.at[i], 1)

        def a_along_z(self, step, offset):
            self.along_z(
                part_a(yn(offset), zt(-step)), step, lambda i: az_sem.at[i, offset % NY],
                -1 if offset in (0, 1) else 1,
            )

        def turn_y(self, step):
            for s in (1, -1):
                ref = part_b(y, zt(-step))
                self.go(ref, by_sem.at[step % NZ, 0 if s > 0 else 1], dev(x, c, yn(s), z))

        def b_along_y(self, step):
            left, right = part_b(yn(-1), zt(-step)), part_b(yn(1), zt(-step))
            arrived(left, by_sem.at[step % NZ, 0])
            arrived(right, by_sem.at[step % NZ, 1])
            sem = by_sem.at[step % NZ, 2]
            if step in (0, 3, 1, -2):
                self.go(left, sem, dev(x, c, yn(1), z))
            else:
                self.go(right, sem, dev(x, c, yn(-1), z))

        def b_end(self, step):
            arrived(part_b(yn(2), zt(-step)), by_sem.at[step % NZ, 2])

    def owner_part():
        for src in range(NY):
            for k in range(2):
                arrived(vr.at[src, pl.ds(k * feats, feats)], v_sem.at[src, k])
        combos = [(a, b) for a in range(NY) for b in range(a, NY)]
        zero = jnp.zeros((8, 128), jnp.float32)

        def products(i, sums):
            rows = pl.ds(pl.multiple_of(i * 16, 16), 16)
            parts = [vr[r, rows, :].astype(jnp.float32) for r in range(NY)]
            return tuple(
                total + lane_sums(parts[a] * parts[b]) for (a, b), total in zip(combos, sums)
            )

        sums = lax.fori_loop(0, block // 16, products, (zero,) * len(combos))
        out_row = lax.broadcasted_iota(jnp.int32, (8, 128), 0) % NY
        out_col = lax.broadcasted_iota(jnp.int32, (8, 128), 1) % NY
        gram = zero
        for (a, b), total in zip(combos, sums):
            value = jnp.sum(total, axis=(0, 1), keepdims=True)
            spot = ((out_row == a) & (out_col == b)) | ((out_row == b) & (out_col == a))
            gram = jnp.where(spot, value, gram)
        me = x * NY + y
        b1[me] = gram
        for s in range(NX):
            for t in range(NY):
                if s or t:
                    send(b1.at[me], b1.at[me], ar_sem.at[2], dev(xn(s), c, yn(t), z), group=7)
        settle()
        arrived(b1.at[pl.ds(0, NX * NY - 1)], ar_sem.at[2])
        b2[z] = jnp.sum(b1[...], axis=0)
        for s in range(1, NZ):
            send(b2.at[z], b2.at[z], ar_sem.at[3], dev(x, zn(s) // 2 % 2, y, zn(s)), group=8)
        arrived(b1.at[pl.ds(0, NX * NY - 1)], group_sem.at[7])
        arrived(b2.at[pl.ds(0, NZ - 1)], ar_sem.at[3])
        last = tree_weights(jnp.sum(b2[...], axis=0), (2, 1))
        side, n = kind_of(z), z // 4
        span = span_of(n)

        def final_rows(i, carry):
            total = jnp.zeros((small, cols), jnp.float32)
            rows = pl.ds(pl.multiple_of(i * small, small), small)
            for r in range(NY):
                total += last[r:r + 1, :] * vr[r, rows, :].astype(jnp.float32)
            out[y, side, rows, span] = total.astype(jnp.bfloat16)
            return carry

        lax.fori_loop(0, block // small, final_rows, 0)
        arrived(b2.at[pl.ds(0, NZ - 1)], group_sem.at[8])
        Gather().run(OWNER_EVENTS)

    def other_part():
        settle()
        arrived(vs.at[0], send_sem.at[last_push])
        Gather().run(OTHER_EVENTS)

    pl.when(is_owner)(owner_part)
    pl.when(jnp.logical_not(is_owner))(other_part)


def on_device(tokens, pre_act, act_grad):
    tok, feat = tokens.shape
    width = pre_act.shape[1]
    feats, cols = feat // 2, width // 2
    rows = feats * NX
    bf16, f32 = jnp.bfloat16, jnp.float32
    dma = pltpu.SemaphoreType.DMA
    combined = pl.pallas_call(
        kernel,
        out_shape=pltpu.VMEM((NX, 2, feat, width), bf16),
        in_specs=[
            pl.BlockSpec(memory_space=pl.ANY),
            pl.BlockSpec(memory_space=pl.ANY),
            pl.BlockSpec(memory_space=pl.ANY),
        ],
        out_specs=pl.BlockSpec(memory_space=pltpu.VMEM),
        scratch_shapes=[
            pltpu.VMEM((NZ, NX, feats, tok), bf16),
            pltpu.VMEM((NZ, tok, cols), bf16),
            pltpu.VMEM((2, tok, cols), bf16),
            pltpu.VMEM((tok, width), bf16),
            pltpu.VMEM((tok, width), bf16),
            pltpu.VMEM((NZ, rows, cols), bf16),
            pltpu.VMEM((NZ, NZ, 8, 128), f32),
            pltpu.VMEM((NY, feats, cols), bf16),
            pltpu.VMEM((NY, 2 * feats, cols), bf16),
            pltpu.VMEM((2 * NX, 8, 128), f32),
            pltpu.VMEM((NZ, 8, 128), f32),
            pltpu.VMEM((NX * NY, 8, 128), f32),
            pltpu.VMEM((NZ, 8, 128), f32),
            dma((2,)),
            dma((SEND_SEMS,)),
            dma((9,)),
            dma((NZ,)),
            dma((NZ, 4)),
            dma((NZ,)),
            dma((NZ,)),
            dma((NY, 2)),
            dma((4,)),
            dma((NZ,)),
            dma((NZ, 3)),
            dma((NZ, NY)),
            dma((4,)),
        ],
        compiler_params=pltpu.CompilerParams(
            collective_id=0, has_side_effects=True, vmem_limit_bytes=52 * 1024 * 1024
        ),
    )(tokens.T, pre_act, act_grad)
    return combined.reshape(feat * 2 * NX, width)


def solution(mesh):
    return jax.shard_map(
        on_device,
        mesh=mesh,
        in_specs=(P("dp", "tp"), P("dp", "tp"), P("dp", "tp")),
        out_specs=P(None, "tp"),
        check_vma=False,
    )
```

```python
import jax
import jax.numpy as jnp
from jax import lax
from jax.experimental import pallas as pl
from jax.experimental.pallas import tpu as pltpu
from jax.sharding import PartitionSpec as P

norm_epsilon = 1e-06
gelu_scale = 0.7978845608
MESH = pl.DeviceIdType.MESH
NX, NY, NZ = 4, 4, 8
SEND_SEMS = 80

OWNER_EVENTS = [
    ("source_y",), ("source_z",), ("first_z", 0), ("turn_y", 0), ("pass_y",), ("first_z", -1),
    ("b_along_z", -1), ("turn_y", -1), ("last_y",), ("first_z", 2), ("first_z", 1), ("b_along_y", 0),
    ("a_along_z", -1, 2), ("b_along_y", -1), ("a_along_z", -1, 0), ("a_along_z", -1, 1), ("b_along_z", 3),
    ("a_along_z", -1, -1), ("turn_y", 3), ("b_along_z", 4), ("b_end", -1), ("b_end", 0), ("turn_y", 4),
    ("a_along_z", 3, -1), ("a_along_z", 3, 2), ("b_along_y", 3), ("b_along_y", 4), ("a_along_z", 4, 0),
    ("a_along_z", 4, 1), ("a_along_z", 3, 1), ("a_along_z", 4, 2), ("b_end", 3), ("a_along_z", 3, 0),
    ("a_along_z", 4, -1), ("b_end", 4),
]
OTHER_EVENTS = [
    ("b_along_z", 1), ("turn_y", 1), ("b_along_z", -2), ("turn_y", -2), ("b_along_z", 2), ("turn_y", 2),
    ("a_along_z", 1, 2), ("a_along_z", 1, 1), ("a_along_z", 1, -1), ("a_along_z", 1, 0), ("a_along_z", 2, 0),
    ("b_along_z", -3), ("b_along_y", 1), ("turn_y", -3), ("a_along_z", -2, 1), ("a_along_z", -2, 2),
    ("b_along_y", 2), ("a_along_z", 2, -1), ("a_along_z", 2, 1), ("a_along_z", -2, -1), ("b_end", 1),
    ("a_along_z", 2, 2), ("a_along_z", -3, 0), ("b_along_y", -2), ("b_along_y", -3), ("a_along_z", -3, -1),
    ("a_along_z", -2, 0), ("a_along_z", -3, 1), ("a_along_z", -3, 2), ("b_end", 2), ("b_end", -3),
    ("b_end", -2),
]


def gelu_slope(values):
    inner = gelu_scale * (values + 0.044715 * values * values * values)
    tangent = jnp.tanh(inner)
    return 0.5 * (1.0 + tangent) + 0.5 * values * (1.0 - tangent * tangent) * gelu_scale * (
        1.0 + 0.134145 * values * values
    )


def tree_weights(gram, strides):
    shape = gram.shape
    row = lax.broadcasted_iota(jnp.int32, shape, 0)
    lane = lax.broadcasted_iota(jnp.int32, shape, 1)
    own = lane % 8 == row
    first = lane < 8
    weight = jnp.ones((8, 1), jnp.float32)
    for stride in strides:
        pair = lane % 8 == (row + stride) % 8
        own_col = jnp.sum(jnp.where(own & first, gram, 0.0), axis=1, keepdims=True)
        pair_col = jnp.sum(jnp.where(pair & first, gram, 0.0), axis=1, keepdims=True)
        own_row = jnp.sum(jnp.where(own, gram, 0.0), axis=0, keepdims=True)
        pair_row = jnp.sum(
            jnp.where(row == (lane + stride) % 8, gram, 0.0), axis=0, keepdims=True
        )
        coef_col = 1.0 - pair_col / (2.0 * (jnp.maximum(own_col, 0.0) + norm_epsilon))
        coef_row = 1.0 - pair_row / (2.0 * (jnp.maximum(own_row, 0.0) + norm_epsilon))
        weight = weight * coef_col
        scaled = gram * coef_col * coef_row
        scaled = scaled + pltpu.roll(scaled, stride, 0)
        gram = scaled + pltpu.roll(scaled, stride, 1)
    return weight


def lane_sums(values):
    total = values[:, :128]
    for start in range(128, values.shape[1], 128):
        total = total + values[:, start:start + 128]
    return total[:8] + total[8:]


def kernel(
    xt, pre, act, out,
    xb, yb, ys, pre_v, act_v, grads, vs, vr,
    a1, a2, b1, b2,
    load_sem, send_sem, group_sem, xz_sem, xx_sem, yz_sem, yy_sem, v_sem, ar_sem,
    bz_sem, by_sem, az_sem, ay_sem,
):
    dp, tp = lax.axis_index("dp"), lax.axis_index("tp")
    z, y, x, c = dp // NY, dp % NY, tp // 2, tp % 2
    toward = 1 - 2 * (z % 2)
    kind = (z + 1) // 2 % 2
    tokens = yb.shape[1]
    half_tok = tokens // 2
    feats = xb.shape[2]
    cols = yb.shape[2]

    def dev(x_, c_, y_, z_):
        return (z_ * NY + y_, x_ * 2 + c_)

    def zn(step):
        return (z + step + NZ) % NZ

    def zt(step):
        return zn(step * toward)

    def yn(step):
        return (y + step + NY) % NY

    def xn(step):
        return (x + step + NX) % NX

    pending = []
    counter = [0]

    def send(src, dst, recv, device, cond=None, group=None, waits=pending):
        if group is None:
            sent = send_sem.at[counter[0]]
            waits.append((src, counter[0], cond))
            counter[0] += 1
        else:
            sent = group_sem.at[group]
        copy = pltpu.make_async_remote_copy(
            src_ref=src, dst_ref=dst, send_sem=sent, recv_sem=recv,
            device_id=device, device_id_type=MESH,
        )
        if cond is None:
            copy.start()
        else:
            pl.when(cond)(copy.start)

    def arrived(ref, sem):
        pltpu.make_async_copy(ref, ref, sem).wait()

    def drain(items):
        for ref, index, cond in items:
            if cond is None:
                arrived(ref, send_sem.at[index])
            else:
                pl.when(cond)(lambda: arrived(ref, send_sem.at[index]))

    loads = [
        pltpu.make_async_copy(pre, pre_v, load_sem.at[0]),
        pltpu.make_async_copy(act, act_v, load_sem.at[1]),
    ]
    for load in loads:
        load.start()

    barrier = pltpu.get_barrier_semaphore()
    partners = [dev(x, k, y, zn(s)) for s in range(1, NZ) for k in range(2)]
    partners += [dev(x, 1 - c, y, z)]
    partners += [dev(xn(s), k, y, z) for s in range(1, NX) for k in range(2)]
    partners += [dev(x, k, yn(s), z) for s in range(1, NY) for k in range(2)]
    partners += [dev(xn(s), c, yn(t), z) for s in range(1, NX) for t in range(1, NY)]
    for partner in partners:
        pl.semaphore_signal(barrier, inc=1, device_id=partner, device_id_type=MESH)
    pl.semaphore_wait(barrier, len(partners))

    match = kind == c
    for near, far in ((-1, 3), (1, -2)):
        cond = match if near < 0 else jnp.logical_not(match)
        for k in range(2):
            rows = xt.at[pl.ds(k * feats, feats)]
            send(rows, xb.at[z, x], xz_sem.at[z], dev(x, k, y, zt(far)), cond, group=0)
            send(rows, xb.at[z, x], xz_sem.at[z], dev(x, k, y, zt(near)), cond, group=0)
    other = pl.multiple_of((1 - c) * feats, 16)
    mine = pl.multiple_of(c * feats, 16)
    own_x = pltpu.make_async_copy(xt.at[pl.ds(mine, feats)], xb.at[z, x], xz_sem.at[z])
    pl.when(match)(own_x.start)
    send(xt.at[pl.ds(other, feats)], xb.at[z, x], xz_sem.at[z], dev(x, 1 - c, y, z), match)

    chunk = 32
    my_pair, my_parity = z // 2, z % 2
    first = jnp.where((c - my_pair + 4) % 4 == 0, 1, 0)

    def ev_sl(turn):
        if turn == 0:
            for load in loads:
                load.wait()
        j = first if turn == 0 else 1 - first
        span = pl.ds(pl.multiple_of(j * cols, 128), cols)

        def slope_rows(i, carry):
            rows = pl.ds(pl.multiple_of(i * chunk, chunk), chunk)
            slope = gelu_slope(pre_v[rows, span].astype(jnp.float32))
            ys[turn, rows, :] = (act_v[rows, span].astype(jnp.float32) * slope).astype(jnp.bfloat16)
            return carry

        lax.fori_loop(0, tokens // chunk, slope_rows, 0)

    def ev_ys(turn):
        pair = c + 2 * (first if turn == 0 else 1 - first)
        ahead = (pair - my_pair + 4) % 4
        upper = jnp.where(
            ahead == 0, 1 - my_parity,
            jnp.where(ahead == 3, 1, jnp.where(ahead == 2, 1 - my_parity, 0)),
        )
        target = 2 * pair + upper
        for k in range(2):
            rows = pl.ds(k * half_tok, half_tok)
            send(ys.at[turn, rows], yb.at[z, rows], yz_sem.at[z], dev(x, k, y, target), group=2)
        own = ahead == 0
        own_rows = pl.ds(pl.multiple_of(c * half_tok, 16), half_tok)
        other_rows = pl.ds(pl.multiple_of((1 - c) * half_tok, 16), half_tok)
        own_y = pltpu.make_async_copy(ys.at[turn, own_rows], yb.at[z, own_rows], yz_sem.at[z])
        pl.when(own)(own_y.start)
        send(ys.at[turn, other_rows], yb.at[z, other_rows], yz_sem.at[z], dev(x, 1 - c, y, z), own)

    def ev_xz(step):
        src = zt(step)
        piece = xb.at[src, x]
        arrived(piece, xz_sem.at[src])
        if step in (1, 2, 3):
            send(piece, piece, xz_sem.at[src], dev(x, c, y, zt(-1)), group=1)
        send(piece, piece, xx_sem.at[src, 0], dev(xn(1), c, y, z), group=0)
        send(piece, piece, xx_sem.at[src, 1], dev(xn(-1), c, y, z), group=0)

    low, high = pl.ds(0, feats // 2), pl.ds(feats // 2, feats // 2)

    def ev_xx(step):
        src = zt(step)
        left, right = xb.at[src, xn(-1)], xb.at[src, xn(1)]
        arrived(left, xx_sem.at[src, 0])
        send(left.at[low], left.at[low], xx_sem.at[src, 2], dev(xn(1), c, y, z), group=0)
        arrived(right, xx_sem.at[src, 1])
        send(right.at[high], right.at[high], xx_sem.at[src, 3], dev(xn(-1), c, y, z), group=0)

    my_tok = pl.ds(pl.multiple_of(c * half_tok, 16), half_tok)
    its_tok = pl.ds(pl.multiple_of((1 - c) * half_tok, 16), half_tok)

    def ev_yz(step):
        src = zt(step)
        piece = yb.at[src, my_tok]
        arrived(piece, yz_sem.at[src])
        if step in (-1, -2, -3):
            send(piece, piece, yz_sem.at[src], dev(x, c, y, zt(1)), group=3 if step == -3 else 2)
        send(piece, piece, yy_sem.at[src], dev(x, 1 - c, y, z), group=2)

    def ev_mm(step):
        src = zt(step)
        far = xb.at[src, xn(2)]
        arrived(far.at[low], xx_sem.at[src, 2])
        arrived(far.at[high], xx_sem.at[src, 3])
        arrived(yb.at[src, its_tok], yy_sem.at[src])

        def block(i, carry):
            result = jnp.dot(xb[src, i], yb[src], preferred_element_type=jnp.float32)
            grads[src, pl.ds(pl.multiple_of(i * feats, 16), feats), :] = result.astype(
                jnp.bfloat16
            ).astype(jnp.float32)
            return carry

        lax.fori_loop(0, NX, block, 0)
        done.append(src)

        def products(i, sums):
            rows = pl.ds(pl.multiple_of(i * 16, 16), 16)
            new = grads[src, rows, :]
            return tuple(
                total + lane_sums(new * (new if old is src else grads[old, rows, :]))
                for old, total in zip(done, sums)
            )

        zero = jnp.zeros((8, 128), jnp.float32)
        sums = lax.fori_loop(0, grads.shape[1] // 16, products, (zero,) * len(done))
        for old, total in zip(done, sums):
            value = jnp.sum(total, axis=(0, 1), keepdims=True)
            spot = ((lead == src) & (tail == old)) | ((lead == old) & (tail == src))
            gram[0] = jnp.where(spot, value, gram[0])

    done = []
    gram = [jnp.zeros((8, 128), jnp.float32)]
    lead = lax.broadcasted_iota(jnp.int32, (8, 128), 0)
    tail = lax.broadcasted_iota(jnp.int32, (8, 128), 1) % NZ
    xz, xx, yz, mm = ev_xz, ev_xx, ev_yz, ev_mm
    sl, yt = ev_sl, ev_ys
    for event, step in [
        (xz, 0), (sl, 0), (xz, -1), (xz, 1), (sl, 1), (xx, 0), (xz, 2), (xz, 3), (yt, 0), (yt, 1),
        (xx, -1), (xx, 1), (xz, -2), (xz, -3), (xx, 2), (xz, 4), (yz, 0), (yz, 1), (yz, -1), (xx, 3), (xx, -2), (xx, -3),
        (mm, 0), (yz, -2), (xx, 4), (mm, 1), (yz, -3), (mm, -1), (yz, 2), (mm, -2), (yz, 3),
        (mm, 2), (mm, -3), (yz, 4), (mm, 3), (mm, 4),
    ]:
        event(step)

    a1[tp] = gram[0]
    for s in range(1, 2 * NX):
        send(a1.at[tp], a1.at[tp], ar_sem.at[0], (dp, (tp + s) % (2 * NX)), group=4)
    arrived(xb.at[pl.ds(0, 7)], group_sem.at[0])
    arrived(xb.at[0, pl.ds(0, 3)], group_sem.at[1])
    arrived(yb.at[pl.ds(0, 7)], group_sem.at[2])
    arrived(yb.at[0, pl.ds(0, half_tok)], group_sem.at[3])
    drain(pending)
    pending.clear()
    sent = pl.ds(0, 2 * NX - 1)
    arrived(a1.at[sent], ar_sem.at[0])
    a2[z] = jnp.sum(a1[...], axis=0)
    for s in range(1, NZ):
        send(a2.at[z], a2.at[z], ar_sem.at[1], dev(x, c, y, zn(s)), group=5)
    arrived(a1.at[sent], group_sem.at[4])
    arrived(a2.at[pl.ds(0, NZ - 1)], ar_sem.at[1])
    weight = tree_weights(jnp.sum(a2[...], axis=0), (4, 2, 1))

    owner = z // 2 % 2
    is_owner = c == owner
    its_rows = pl.ds(pl.multiple_of(c * feats, 16), feats)
    small = 32
    for s in (1, -1, 2, 0):
        part = yn(s)

        def combine_rows(i, carry):
            total = jnp.zeros((small, cols), jnp.float32)
            rows = pl.ds(pl.multiple_of(part * feats + i * small, 32), small)
            for r in range(NZ):
                total += weight[r:r + 1, :] * grads[r, rows, :]
            vs[part, pl.ds(pl.multiple_of(i * small, small), small), :] = total.astype(jnp.bfloat16)
            return carry

        lax.fori_loop(0, feats // small, combine_rows, 0)
        if s:
            send(vs.at[part], vr.at[y, its_rows], v_sem.at[y, c], dev(x, owner, part, z), group=6)
        else:
            own_v = pltpu.make_async_copy(vs.at[part], vr.at[y, its_rows], v_sem.at[y, c])
            pl.when(is_owner)(own_v.start)
            last_push = counter[0]
            send(vs.at[part], vr.at[y, its_rows], v_sem.at[y, c], dev(x, owner, part, z),
                 jnp.logical_not(is_owner))
            pending.clear()

    def settle():
        arrived(a2.at[pl.ds(0, NZ - 1)], group_sem.at[5])
        arrived(vs.at[pl.ds(0, NY - 1)], group_sem.at[6])

    block = 2 * feats
    cut = block * 2 // 5
    rest = block - cut

    def kind_of(z_):
        return (z_ + 1) // 2 % 2

    def span_of(n):
        return pl.ds(pl.multiple_of(n * cols, 128), cols)

    def part_a(y_, src, start=0, size=cut):
        return out.at[y_, kind_of(src), pl.ds(start, size), span_of(src // 4)]

    def part_b(y_, src):
        return out.at[y_, kind_of(src), pl.ds(cut, rest), span_of(src // 4)]

    class Gather:
        def __init__(self):
            self.waits = []

        def run(self, events):
            for name, *args in events:
                getattr(self, name)(*args)
            drain(self.waits)

        def go(self, ref, sem, device):
            send(ref, ref, sem, device, waits=self.waits)

        def source_z(self):
            for s in (1, -1):
                self.go(part_b(y, z), bz_sem.at[-s % NZ], dev(x, c, y, zt(s)))

        def source_y(self):
            for s in (1, -1):
                self.go(part_a(y, z), ay_sem.at[0 if s > 0 else 1], dev(x, c, yn(s), z))

        def pass_y(self):
            half = cut // 2
            arrived(part_a(yn(-1), z), ay_sem.at[0])
            self.go(part_a(yn(-1), z, 0, half), ay_sem.at[2], dev(x, c, yn(1), z))
            arrived(part_a(yn(1), z), ay_sem.at[1])
            self.go(part_a(yn(1), z, half, half), ay_sem.at[3], dev(x, c, yn(-1), z))

        def last_y(self):
            half = cut // 2
            arrived(part_a(yn(2), z, 0, half), ay_sem.at[2])
            arrived(part_a(yn(2), z, half, half), ay_sem.at[3])

        def first_z(self, offset):
            for s in (1, -1):
                self.go(part_a(yn(offset), z), az_sem.at[-s % NZ, offset % NY], dev(x, c, y, zt(s)))

        def along_z(self, ref, step, sem_at, opposite):
            arrived(ref, sem_at(step % NZ))
            sign = 1 if step > 0 else -1
            if abs(step) < 3 or (abs(step) == 3 and sign == opposite):
                self.go(ref, sem_at(-(step + sign) % NZ), dev(x, c, y, zt(sign)))

        def b_along_z(self, step):
            self.along_z(part_b(y, zt(-step)), step, lambda i: bz_sem.at[i], 1)

        def a_along_z(self, step, offset):
            self.along_z(
                part_a(yn(offset), zt(-step)), step, lambda i: az_sem.at[i, offset % NY],
                -1 if offset in (0, 1) else 1,
            )

        def turn_y(self, step):
            for s in (1, -1):
                ref = part_b(y, zt(-step))
                self.go(ref, by_sem.at[step % NZ, 0 if s > 0 else 1], dev(x, c, yn(s), z))

        def b_along_y(self, step):
            left, right = part_b(yn(-1), zt(-step)), part_b(yn(1), zt(-step))
            arrived(left, by_sem.at[step % NZ, 0])
            arrived(right, by_sem.at[step % NZ, 1])
            sem = by_sem.at[step % NZ, 2]
            if step in (0, 3, 1, -2):
                self.go(left, sem, dev(x, c, yn(1), z))
            else:
                self.go(right, sem, dev(x, c, yn(-1), z))

        def b_end(self, step):
            arrived(part_b(yn(2), zt(-step)), by_sem.at[step % NZ, 2])

    def owner_part():
        for src in range(NY):
            for k in range(2):
                arrived(vr.at[src, pl.ds(k * feats, feats)], v_sem.at[src, k])
        combos = [(a, b) for a in range(NY) for b in range(a, NY)]
        zero = jnp.zeros((8, 128), jnp.float32)

        def products(i, sums):
            rows = pl.ds(pl.multiple_of(i * 16, 16), 16)
            parts = [vr[r, rows, :].astype(jnp.float32) for r in range(NY)]
            return tuple(
                total + lane_sums(parts[a] * parts[b]) for (a, b), total in zip(combos, sums)
            )

        sums = lax.fori_loop(0, block // 16, products, (zero,) * len(combos))
        out_row = lax.broadcasted_iota(jnp.int32, (8, 128), 0) % NY
        out_col = lax.broadcasted_iota(jnp.int32, (8, 128), 1) % NY
        gram = zero
        for (a, b), total in zip(combos, sums):
            value = jnp.sum(total, axis=(0, 1), keepdims=True)
            spot = ((out_row == a) & (out_col == b)) | ((out_row == b) & (out_col == a))
            gram = jnp.where(spot, value, gram)
        me = x * NY + y
        b1[me] = gram
        for s in range(NX):
            for t in range(NY):
                if s or t:
                    send(b1.at[me], b1.at[me], ar_sem.at[2], dev(xn(s), c, yn(t), z), group=7)
        settle()
        arrived(b1.at[pl.ds(0, NX * NY - 1)], ar_sem.at[2])
        b2[z] = jnp.sum(b1[...], axis=0)
        for s in range(1, NZ):
            send(b2.at[z], b2.at[z], ar_sem.at[3], dev(x, zn(s) // 2 % 2, y, zn(s)), group=8)
        arrived(b1.at[pl.ds(0, NX * NY - 1)], group_sem.at[7])
        arrived(b2.at[pl.ds(0, NZ - 1)], ar_sem.at[3])
        last = tree_weights(jnp.sum(b2[...], axis=0), (2, 1))
        side, n = kind_of(z), z // 4
        span = span_of(n)

        def final_rows(i, carry):
            total = jnp.zeros((small, cols), jnp.float32)
            rows = pl.ds(pl.multiple_of(i * small, small), small)
            for r in range(NY):
                total += last[r:r + 1, :] * vr[r, rows, :].astype(jnp.float32)
            out[y, side, rows, span] = total.astype(jnp.bfloat16)
            return carry

        lax.fori_loop(0, block // small, final_rows, 0)
        arrived(b2.at[pl.ds(0, NZ - 1)], group_sem.at[8])
        Gather().run(OWNER_EVENTS)

    def other_part():
        settle()
        arrived(vs.at[0], send_sem.at[last_push])
        Gather().run(OTHER_EVENTS)

    pl.when(is_owner)(owner_part)
    pl.when(jnp.logical_not(is_owner))(other_part)


def on_device(tokens, pre_act, act_grad):
    tok, feat = tokens.shape
    width = pre_act.shape[1]
    feats, cols = feat // 2, width // 2
    rows = feats * NX
    bf16, f32 = jnp.bfloat16, jnp.float32
    dma = pltpu.SemaphoreType.DMA
    combined = pl.pallas_call(
        kernel,
        out_shape=pltpu.VMEM((NX, 2, feat, width), bf16),
        in_specs=[
            pl.BlockSpec(memory_space=pl.ANY),
            pl.BlockSpec(memory_space=pl.ANY),
            pl.BlockSpec(memory_space=pl.ANY),
        ],
        out_specs=pl.BlockSpec(memory_space=pltpu.VMEM),
        scratch_shapes=[
            pltpu.VMEM((NZ, NX, feats, tok), bf16),
            pltpu.VMEM((NZ, tok, cols), bf16),
            pltpu.VMEM((2, tok, cols), bf16),
            pltpu.VMEM((tok, width), bf16),
            pltpu.VMEM((tok, width), bf16),
            pltpu.VMEM((NZ, rows, cols), f32),
            pltpu.VMEM((NY, feats, cols), bf16),
            pltpu.VMEM((NY, 2 * feats, cols), bf16),
            pltpu.VMEM((2 * NX, 8, 128), f32),
            pltpu.VMEM((NZ, 8, 128), f32),
            pltpu.VMEM((NX * NY, 8, 128), f32),
            pltpu.VMEM((NZ, 8, 128), f32),
            dma((2,)),
            dma((SEND_SEMS,)),
            dma((9,)),
            dma((NZ,)),
            dma((NZ, 4)),
            dma((NZ,)),
            dma((NZ,)),
            dma((NY, 2)),
            dma((4,)),
            dma((NZ,)),
            dma((NZ, 3)),
            dma((NZ, NY)),
            dma((4,)),
        ],
        compiler_params=pltpu.CompilerParams(
            collective_id=0, has_side_effects=True, vmem_limit_bytes=52 * 1024 * 1024
        ),
    )(tokens.T, pre_act, act_grad)
    return combined.reshape(feat * 2 * NX, width)


def solution(mesh):
    return jax.shard_map(
        on_device,
        mesh=mesh,
        in_specs=(P("dp", "tp"), P("dp", "tp"), P("dp", "tp")),
        out_specs=P(None, "tp"),
        check_vma=False,
    )
```

```python
import jax
import jax.numpy as jnp
from jax import lax
from jax.experimental import pallas as pl
from jax.experimental.pallas import tpu as pltpu
from jax.sharding import PartitionSpec as P

norm_epsilon = 1e-06
gelu_scale = 0.7978845608
MESH = pl.DeviceIdType.MESH
NX, NY, NZ = 4, 4, 8
SEND_SEMS = 80

OWNER_EVENTS = [
    ("source_y",), ("source_z",), ("first_z", 0), ("turn_y", 0), ("pass_y",), ("first_z", -1),
    ("b_along_z", -1), ("turn_y", -1), ("last_y",), ("first_z", 2), ("first_z", 1), ("b_along_y", 0),
    ("a_along_z", -1, 2), ("b_along_y", -1), ("a_along_z", -1, 0), ("a_along_z", -1, 1), ("b_along_z", 3),
    ("a_along_z", -1, -1), ("turn_y", 3), ("b_along_z", 4), ("b_end", -1), ("b_end", 0), ("turn_y", 4),
    ("a_along_z", 3, -1), ("a_along_z", 3, 2), ("b_along_y", 3), ("b_along_y", 4), ("a_along_z", 4, 0),
    ("a_along_z", 4, 1), ("a_along_z", 3, 1), ("a_along_z", 4, 2), ("b_end", 3), ("a_along_z", 3, 0),
    ("a_along_z", 4, -1), ("b_end", 4),
]
OTHER_EVENTS = [
    ("b_along_z", 1), ("turn_y", 1), ("b_along_z", -2), ("turn_y", -2), ("b_along_z", 2), ("turn_y", 2),
    ("a_along_z", 1, 2), ("a_along_z", 1, 1), ("a_along_z", 1, -1), ("a_along_z", 1, 0), ("a_along_z", 2, 0),
    ("b_along_z", -3), ("b_along_y", 1), ("turn_y", -3), ("a_along_z", -2, 1), ("a_along_z", -2, 2),
    ("b_along_y", 2), ("a_along_z", 2, -1), ("a_along_z", 2, 1), ("a_along_z", -2, -1), ("b_end", 1),
    ("a_along_z", 2, 2), ("a_along_z", -3, 0), ("b_along_y", -2), ("b_along_y", -3), ("a_along_z", -3, -1),
    ("a_along_z", -2, 0), ("a_along_z", -3, 1), ("a_along_z", -3, 2), ("b_end", 2), ("b_end", -3),
    ("b_end", -2),
]


def gelu_slope(values):
    inner = gelu_scale * (values + 0.044715 * values * values * values)
    tangent = jnp.tanh(inner)
    return 0.5 * (1.0 + tangent) + 0.5 * values * (1.0 - tangent * tangent) * gelu_scale * (
        1.0 + 0.134145 * values * values
    )


def tree_weights(gram, strides):
    shape = gram.shape
    row = lax.broadcasted_iota(jnp.int32, shape, 0)
    lane = lax.broadcasted_iota(jnp.int32, shape, 1)
    own = lane % 8 == row
    first = lane < 8
    weight = jnp.ones((8, 1), jnp.float32)
    for stride in strides:
        pair = lane % 8 == (row + stride) % 8
        own_col = jnp.sum(jnp.where(own & first, gram, 0.0), axis=1, keepdims=True)
        pair_col = jnp.sum(jnp.where(pair & first, gram, 0.0), axis=1, keepdims=True)
        own_row = jnp.sum(jnp.where(own, gram, 0.0), axis=0, keepdims=True)
        pair_row = jnp.sum(
            jnp.where(row == (lane + stride) % 8, gram, 0.0), axis=0, keepdims=True
        )
        coef_col = 1.0 - pair_col / (2.0 * (jnp.maximum(own_col, 0.0) + norm_epsilon))
        coef_row = 1.0 - pair_row / (2.0 * (jnp.maximum(own_row, 0.0) + norm_epsilon))
        weight = weight * coef_col
        scaled = gram * coef_col * coef_row
        scaled = scaled + pltpu.roll(scaled, stride, 0)
        gram = scaled + pltpu.roll(scaled, stride, 1)
    return weight


def lane_sums(values):
    total = values[:, :128]
    for start in range(128, values.shape[1], 128):
        total = total + values[:, start:start + 128]
    return total[:8] + total[8:]


def kernel(
    xt, pre, act, out,
    xb, yb, ys, pre_v, act_v, grads, vs, vr,
    a1, a2, b1, b2,
    load_sem, send_sem, group_sem, xz_sem, xx_sem, yz_sem, yy_sem, v_sem, ar_sem,
    bz_sem, by_sem, az_sem, ay_sem,
):
    dp, tp = lax.axis_index("dp"), lax.axis_index("tp")
    z, y, x, c = dp // NY, dp % NY, tp // 2, tp % 2
    toward = 1 - 2 * (z % 2)
    kind = (z + 1) // 2 % 2
    tokens = yb.shape[1]
    half_tok = tokens // 2
    feats = xb.shape[2]
    cols = yb.shape[2]

    def dev(x_, c_, y_, z_):
        return (z_ * NY + y_, x_ * 2 + c_)

    def zn(step):
        return (z + step + NZ) % NZ

    def zt(step):
        return zn(step * toward)

    def yn(step):
        return (y + step + NY) % NY

    def xn(step):
        return (x + step + NX) % NX

    pending = []
    counter = [0]

    def send(src, dst, recv, device, cond=None, group=None, waits=pending):
        if group is None:
            sent = send_sem.at[counter[0]]
            waits.append((src, counter[0], cond))
            counter[0] += 1
        else:
            sent = group_sem.at[group]
        copy = pltpu.make_async_remote_copy(
            src_ref=src, dst_ref=dst, send_sem=sent, recv_sem=recv,
            device_id=device, device_id_type=MESH,
        )
        if cond is None:
            copy.start()
        else:
            pl.when(cond)(copy.start)

    def arrived(ref, sem):
        pltpu.make_async_copy(ref, ref, sem).wait()

    def drain(items):
        for ref, index, cond in items:
            if cond is None:
                arrived(ref, send_sem.at[index])
            else:
                pl.when(cond)(lambda: arrived(ref, send_sem.at[index]))

    loads = [
        pltpu.make_async_copy(pre, pre_v, load_sem.at[0]),
        pltpu.make_async_copy(act, act_v, load_sem.at[1]),
    ]
    for load in loads:
        load.start()

    barrier = pltpu.get_barrier_semaphore()
    partners = [dev(x, k, y, zn(s)) for s in range(1, NZ) for k in range(2)]
    partners += [dev(x, 1 - c, y, z)]
    partners += [dev(xn(s), k, y, z) for s in range(1, NX) for k in range(2)]
    partners += [dev(x, k, yn(s), z) for s in range(1, NY) for k in range(2)]
    partners += [dev(xn(s), c, yn(t), z) for s in range(1, NX) for t in range(1, NY)]
    for partner in partners:
        pl.semaphore_signal(barrier, inc=1, device_id=partner, device_id_type=MESH)
    pl.semaphore_wait(barrier, len(partners))

    match = kind == c
    for near, far in ((-1, 3), (1, -2)):
        cond = match if near < 0 else jnp.logical_not(match)
        for k in range(2):
            rows = xt.at[pl.ds(k * feats, feats)]
            send(rows, xb.at[z, x], xz_sem.at[z], dev(x, k, y, zt(far)), cond, group=0)
            send(rows, xb.at[z, x], xz_sem.at[z], dev(x, k, y, zt(near)), cond, group=0)
    other = pl.multiple_of((1 - c) * feats, 16)
    mine = pl.multiple_of(c * feats, 16)
    own_x = pltpu.make_async_copy(xt.at[pl.ds(mine, feats)], xb.at[z, x], xz_sem.at[z])
    pl.when(match)(own_x.start)
    send(xt.at[pl.ds(other, feats)], xb.at[z, x], xz_sem.at[z], dev(x, 1 - c, y, z), match)

    chunk = 32
    my_pair, my_parity = z // 2, z % 2
    first = jnp.where((c - my_pair + 4) % 4 == 0, 1, 0)

    def ev_sl(turn):
        if turn == 0:
            for load in loads:
                load.wait()
        j = first if turn == 0 else 1 - first
        span = pl.ds(pl.multiple_of(j * cols, 128), cols)

        def slope_rows(i, carry):
            rows = pl.ds(pl.multiple_of(i * chunk, chunk), chunk)
            slope = gelu_slope(pre_v[rows, span].astype(jnp.float32))
            ys[turn, rows, :] = (act_v[rows, span].astype(jnp.float32) * slope).astype(jnp.bfloat16)
            return carry

        lax.fori_loop(0, tokens // chunk, slope_rows, 0)

    def ev_ys(turn):
        pair = c + 2 * (first if turn == 0 else 1 - first)
        ahead = (pair - my_pair + 4) % 4
        upper = jnp.where(
            ahead == 0, 1 - my_parity,
            jnp.where(ahead == 3, 1, jnp.where(ahead == 2, 1 - my_parity, 0)),
        )
        target = 2 * pair + upper
        for k in range(2):
            rows = pl.ds(k * half_tok, half_tok)
            send(ys.at[turn, rows], yb.at[z, rows], yz_sem.at[z], dev(x, k, y, target), group=2)
        own = ahead == 0
        own_rows = pl.ds(pl.multiple_of(c * half_tok, 16), half_tok)
        other_rows = pl.ds(pl.multiple_of((1 - c) * half_tok, 16), half_tok)
        own_y = pltpu.make_async_copy(ys.at[turn, own_rows], yb.at[z, own_rows], yz_sem.at[z])
        pl.when(own)(own_y.start)
        send(ys.at[turn, other_rows], yb.at[z, other_rows], yz_sem.at[z], dev(x, 1 - c, y, z), own)

    def ev_xz(step):
        src = zt(step)
        piece = xb.at[src, x]
        arrived(piece, xz_sem.at[src])
        if step in (1, 2, 3):
            send(piece, piece, xz_sem.at[src], dev(x, c, y, zt(-1)), group=1)
        send(piece, piece, xx_sem.at[src, 0], dev(xn(1), c, y, z), group=0)
        send(piece, piece, xx_sem.at[src, 1], dev(xn(-1), c, y, z), group=0)

    low, high = pl.ds(0, feats // 2), pl.ds(feats // 2, feats // 2)

    def ev_xx(step):
        src = zt(step)
        left, right = xb.at[src, xn(-1)], xb.at[src, xn(1)]
        arrived(left, xx_sem.at[src, 0])
        send(left.at[low], left.at[low], xx_sem.at[src, 2], dev(xn(1), c, y, z), group=0)
        arrived(right, xx_sem.at[src, 1])
        send(right.at[high], right.at[high], xx_sem.at[src, 3], dev(xn(-1), c, y, z), group=0)

    my_tok = pl.ds(pl.multiple_of(c * half_tok, 16), half_tok)
    its_tok = pl.ds(pl.multiple_of((1 - c) * half_tok, 16), half_tok)

    def ev_yz(step):
        src = zt(step)
        piece = yb.at[src, my_tok]
        arrived(piece, yz_sem.at[src])
        if step in (-1, -2, -3):
            send(piece, piece, yz_sem.at[src], dev(x, c, y, zt(1)), group=3 if step == -3 else 2)
        send(piece, piece, yy_sem.at[src], dev(x, 1 - c, y, z), group=2)

    def ev_mm(step):
        src = zt(step)
        far = xb.at[src, xn(2)]
        arrived(far.at[low], xx_sem.at[src, 2])
        arrived(far.at[high], xx_sem.at[src, 3])
        arrived(yb.at[src, its_tok], yy_sem.at[src])

        def block(i, carry):
            result = jnp.dot(xb[src, i], yb[src], preferred_element_type=jnp.float32)
            grads[src, pl.ds(pl.multiple_of(i * feats, 16), feats), :] = result.astype(
                jnp.bfloat16
            ).astype(jnp.float32)
            return carry

        lax.fori_loop(0, NX, block, 0)
        done.append(src)

        def products(i, sums):
            rows = pl.ds(pl.multiple_of(i * 16, 16), 16)
            new = grads[src, rows, :]
            return tuple(
                total + lane_sums(new * (new if old is src else grads[old, rows, :]))
                for old, total in zip(done, sums)
            )

        zero = jnp.zeros((8, 128), jnp.float32)
        sums = lax.fori_loop(0, grads.shape[1] // 16, products, (zero,) * len(done))
        for old, total in zip(done, sums):
            value = jnp.sum(total, axis=(0, 1), keepdims=True)
            spot = ((lead == src) & (tail == old)) | ((lead == old) & (tail == src))
            gram[0] = jnp.where(spot, value, gram[0])

    done = []
    gram = [jnp.zeros((8, 128), jnp.float32)]
    lead = lax.broadcasted_iota(jnp.int32, (8, 128), 0)
    tail = lax.broadcasted_iota(jnp.int32, (8, 128), 1) % NZ
    xz, xx, yz, mm = ev_xz, ev_xx, ev_yz, ev_mm
    sl, yt = ev_sl, ev_ys
    for event, step in [
        (xz, 0), (sl, 0), (xz, -1), (xz, 1), (sl, 1), (xx, 0), (xz, 2), (xz, 3), (yt, 0), (yt, 1),
        (xx, -1), (xx, 1), (xz, -2), (xz, -3), (xx, 2), (xz, 4), (yz, 0), (yz, 1), (yz, -1), (xx, 3), (xx, -2), (xx, -3),
        (mm, 0), (yz, -2), (xx, 4), (mm, 1), (yz, -3), (mm, -1), (yz, 2), (mm, -2), (yz, 3),
        (mm, 2), (mm, -3), (yz, 4), (mm, 3), (mm, 4),
    ]:
        event(step)

    a1[tp] = gram[0]
    for s in range(1, 2 * NX):
        send(a1.at[tp], a1.at[tp], ar_sem.at[0], (dp, (tp + s) % (2 * NX)), group=4)
    arrived(xb.at[pl.ds(0, 7)], group_sem.at[0])
    arrived(xb.at[0, pl.ds(0, 3)], group_sem.at[1])
    arrived(yb.at[pl.ds(0, 7)], group_sem.at[2])
    arrived(yb.at[0, pl.ds(0, half_tok)], group_sem.at[3])
    drain(pending)
    pending.clear()
    sent = pl.ds(0, 2 * NX - 1)
    arrived(a1.at[sent], ar_sem.at[0])
    a2[z] = jnp.sum(a1[...], axis=0)
    for s in range(1, NZ):
        send(a2.at[z], a2.at[z], ar_sem.at[1], dev(x, c, y, zn(s)), group=5)
    arrived(a1.at[sent], group_sem.at[4])
    arrived(a2.at[pl.ds(0, NZ - 1)], ar_sem.at[1])
    weight = tree_weights(jnp.sum(a2[...], axis=0), (4, 2, 1))

    owner = z // 2 % 2
    is_owner = c == owner
    its_rows = pl.ds(pl.multiple_of(c * feats, 16), feats)
    small = 32
    for s in (2, 1, -1, 0):
        part = yn(s)

        def combine_rows(i, carry):
            total = jnp.zeros((small, cols), jnp.float32)
            rows = pl.ds(pl.multiple_of(part * feats + i * small, 32), small)
            for r in range(NZ):
                total += weight[r:r + 1, :] * grads[r, rows, :]
            vs[part, pl.ds(pl.multiple_of(i * small, small), small), :] = total.astype(jnp.bfloat16)
            return carry

        lax.fori_loop(0, feats // small, combine_rows, 0)
        if s:
            send(vs.at[part], vr.at[y, its_rows], v_sem.at[y, c], dev(x, owner, part, z), group=6)
        else:
            own_v = pltpu.make_async_copy(vs.at[part], vr.at[y, its_rows], v_sem.at[y, c])
            pl.when(is_owner)(own_v.start)
            last_push = counter[0]
            send(vs.at[part], vr.at[y, its_rows], v_sem.at[y, c], dev(x, owner, part, z),
                 jnp.logical_not(is_owner))
            pending.clear()

    def settle():
        arrived(a2.at[pl.ds(0, NZ - 1)], group_sem.at[5])
        arrived(vs.at[pl.ds(0, NY - 1)], group_sem.at[6])

    block = 2 * feats
    cut = block * 2 // 5
    rest = block - cut

    def kind_of(z_):
        return (z_ + 1) // 2 % 2

    def span_of(n):
        return pl.ds(pl.multiple_of(n * cols, 128), cols)

    def part_a(y_, src, start=0, size=cut):
        return out.at[y_, kind_of(src), pl.ds(start, size), span_of(src // 4)]

    def part_b(y_, src):
        return out.at[y_, kind_of(src), pl.ds(cut, rest), span_of(src // 4)]

    class Gather:
        def __init__(self):
            self.waits = []

        def run(self, events):
            for name, *args in events:
                getattr(self, name)(*args)
            drain(self.waits)

        def go(self, ref, sem, device):
            send(ref, ref, sem, device, waits=self.waits)

        def source_z(self):
            for s in (1, -1):
                self.go(part_b(y, z), bz_sem.at[-s % NZ], dev(x, c, y, zt(s)))

        def source_y(self):
            for s in (1, -1):
                self.go(part_a(y, z), ay_sem.at[0 if s > 0 else 1], dev(x, c, yn(s), z))

        def pass_y(self):
            half = cut // 2
            arrived(part_a(yn(-1), z), ay_sem.at[0])
            self.go(part_a(yn(-1), z, 0, half), ay_sem.at[2], dev(x, c, yn(1), z))
            arrived(part_a(yn(1), z), ay_sem.at[1])
            self.go(part_a(yn(1), z, half, half), ay_sem.at[3], dev(x, c, yn(-1), z))

        def last_y(self):
            half = cut // 2
            arrived(part_a(yn(2), z, 0, half), ay_sem.at[2])
            arrived(part_a(yn(2), z, half, half), ay_sem.at[3])

        def first_z(self, offset):
            for s in (1, -1):
                self.go(part_a(yn(offset), z), az_sem.at[-s % NZ, offset % NY], dev(x, c, y, zt(s)))

        def along_z(self, ref, step, sem_at, opposite):
            arrived(ref, sem_at(step % NZ))
            sign = 1 if step > 0 else -1
            if abs(step) < 3 or (abs(step) == 3 and sign == opposite):
                self.go(ref, sem_at(-(step + sign) % NZ), dev(x, c, y, zt(sign)))

        def b_along_z(self, step):
            self.along_z(part_b(y, zt(-step)), step, lambda i: bz_sem.at[i], 1)

        def a_along_z(self, step, offset):
            self.along_z(
                part_a(yn(offset), zt(-step)), step, lambda i: az_sem.at[i, offset % NY],
                -1 if offset in (0, 1) else 1,
            )

        def turn_y(self, step):
            for s in (1, -1):
                ref = part_b(y, zt(-step))
                self.go(ref, by_sem.at[step % NZ, 0 if s > 0 else 1], dev(x, c, yn(s), z))

        def b_along_y(self, step):
            left, right = part_b(yn(-1), zt(-step)), part_b(yn(1), zt(-step))
            arrived(left, by_sem.at[step % NZ, 0])
            arrived(right, by_sem.at[step % NZ, 1])
            sem = by_sem.at[step % NZ, 2]
            if step in (0, 3, 1, -2):
                self.go(left, sem, dev(x, c, yn(1), z))
            else:
                self.go(right, sem, dev(x, c, yn(-1), z))

        def b_end(self, step):
            arrived(part_b(yn(2), zt(-step)), by_sem.at[step % NZ, 2])

    def owner_part():
        for src in range(NY):
            for k in range(2):
                arrived(vr.at[src, pl.ds(k * feats, feats)], v_sem.at[src, k])
        combos = [(a, b) for a in range(NY) for b in range(a, NY)]
        zero = jnp.zeros((8, 128), jnp.float32)

        def products(i, sums):
            rows = pl.ds(pl.multiple_of(i * 16, 16), 16)
            parts = [vr[r, rows, :].astype(jnp.float32) for r in range(NY)]
            return tuple(
                total + lane_sums(parts[a] * parts[b]) for (a, b), total in zip(combos, sums)
            )

        sums = lax.fori_loop(0, block // 16, products, (zero,) * len(combos))
        out_row = lax.broadcasted_iota(jnp.int32, (8, 128), 0) % NY
        out_col = lax.broadcasted_iota(jnp.int32, (8, 128), 1) % NY
        gram = zero
        for (a, b), total in zip(combos, sums):
            value = jnp.sum(total, axis=(0, 1), keepdims=True)
            spot = ((out_row == a) & (out_col == b)) | ((out_row == b) & (out_col == a))
            gram = jnp.where(spot, value, gram)
        me = x * NY + y
        b1[me] = gram
        for s in range(NX):
            for t in range(NY):
                if s or t:
                    send(b1.at[me], b1.at[me], ar_sem.at[2], dev(xn(s), c, yn(t), z), group=7)
        settle()
        arrived(b1.at[pl.ds(0, NX * NY - 1)], ar_sem.at[2])
        b2[z] = jnp.sum(b1[...], axis=0)
        for s in range(1, NZ):
            send(b2.at[z], b2.at[z], ar_sem.at[3], dev(x, zn(s) // 2 % 2, y, zn(s)), group=8)
        arrived(b1.at[pl.ds(0, NX * NY - 1)], group_sem.at[7])
        arrived(b2.at[pl.ds(0, NZ - 1)], ar_sem.at[3])
        last = tree_weights(jnp.sum(b2[...], axis=0), (2, 1))
        side, n = kind_of(z), z // 4
        span = span_of(n)

        def final_rows(i, carry):
            total = jnp.zeros((small, cols), jnp.float32)
            rows = pl.ds(pl.multiple_of(i * small, small), small)
            for r in range(NY):
                total += last[r:r + 1, :] * vr[r, rows, :].astype(jnp.float32)
            out[y, side, rows, span] = total.astype(jnp.bfloat16)
            return carry

        lax.fori_loop(0, block // small, final_rows, 0)
        arrived(b2.at[pl.ds(0, NZ - 1)], group_sem.at[8])
        Gather().run(OWNER_EVENTS)

    def other_part():
        settle()
        arrived(vs.at[0], send_sem.at[last_push])
        Gather().run(OTHER_EVENTS)

    pl.when(is_owner)(owner_part)
    pl.when(jnp.logical_not(is_owner))(other_part)


def on_device(tokens, pre_act, act_grad):
    tok, feat = tokens.shape
    width = pre_act.shape[1]
    feats, cols = feat // 2, width // 2
    rows = feats * NX
    bf16, f32 = jnp.bfloat16, jnp.float32
    dma = pltpu.SemaphoreType.DMA
    combined = pl.pallas_call(
        kernel,
        out_shape=pltpu.VMEM((NX, 2, feat, width), bf16),
        in_specs=[
            pl.BlockSpec(memory_space=pl.ANY),
            pl.BlockSpec(memory_space=pl.ANY),
            pl.BlockSpec(memory_space=pl.ANY),
        ],
        out_specs=pl.BlockSpec(memory_space=pltpu.VMEM),
        scratch_shapes=[
            pltpu.VMEM((NZ, NX, feats, tok), bf16),
            pltpu.VMEM((NZ, tok, cols), bf16),
            pltpu.VMEM((2, tok, cols), bf16),
            pltpu.VMEM((tok, width), bf16),
            pltpu.VMEM((tok, width), bf16),
            pltpu.VMEM((NZ, rows, cols), f32),
            pltpu.VMEM((NY, feats, cols), bf16),
            pltpu.VMEM((NY, 2 * feats, cols), bf16),
            pltpu.VMEM((2 * NX, 8, 128), f32),
            pltpu.VMEM((NZ, 8, 128), f32),
            pltpu.VMEM((NX * NY, 8, 128), f32),
            pltpu.VMEM((NZ, 8, 128), f32),
            dma((2,)),
            dma((SEND_SEMS,)),
            dma((9,)),
            dma((NZ,)),
            dma((NZ, 4)),
            dma((NZ,)),
            dma((NZ,)),
            dma((NY, 2)),
            dma((4,)),
            dma((NZ,)),
            dma((NZ, 3)),
            dma((NZ, NY)),
            dma((4,)),
        ],
        compiler_params=pltpu.CompilerParams(
            collective_id=0, has_side_effects=True, vmem_limit_bytes=52 * 1024 * 1024
        ),
    )(tokens.T, pre_act, act_grad)
    return combined.reshape(feat * 2 * NX, width)


def solution(mesh):
    return jax.shard_map(
        on_device,
        mesh=mesh,
        in_specs=(P("dp", "tp"), P("dp", "tp"), P("dp", "tp")),
        out_specs=P(None, "tp"),
        check_vma=False,
    )
```
